128 devices in a mesh: band: 16 (over x, z_hi, core), slab: 8 (over y, z_lo).
Axes of the slice: x: 4, y: 4, z: 4 (z_hi: 2, z_lo: 2; z = z_hi * 2 + z_lo), core: 2. Of those that a mesh axis runs over, the one named last changes fastest.
Arguments:
- orbitals: bfloat16 [16, 128, 128, 128], P('band', 'slab'), may hold values from -6 to 6
- projections: bfloat16 [16, 9, 512], P('band'), may hold values from -4 to 4
- aug_blocks: bfloat16 [512, 8, 9, 128], P(('band', 'slab')), may hold values from -3 to 3
- atom_home: int32 [3, 512], replicated, may hold values from 0 to 62, as said below
Outputs:
- exchange_applied: float32 [16, 128, 128, 128], P('band', 'slab')
The draws below stay inside these ranges and needn't reach their ends.
Inputs may be any that keep to these rules, and one draw needn't show every extreme that they name: `atom_home`: row 0 holds an atom's first brick along the first dimension, rows 1 and 2 along the second and third; its box of 2 x 2 x 2 bricks lies inside one slab of 16 planes. `atom_home`: atoms are numbered by device, 4 to a device in mesh order (band first). Of one device's atoms at most 1 lie in one slab, and exactly 1 lie in one slab that is the same for every device.
All inputs are finite; a program needn't handle non-finite values.
Results may differ from the reference program's by a relative error of at most 0.0012.
Values may be sent and summed in bfloat16 or wider, within the bound.
No kernel may reach another device: no remote copies, remote signals or barrier semaphores. Data moves between devices by JAX's collectives and lax.ppermute only.
A program may use at most 192 MiB of HBM per device.

```python
import math
import jax
import jax.numpy as jnp
from jax import lax

NG = 128
NB = 1
ATOM_DEV = 4
NCH = 9
NBRK = 8
BRICK = 128
BANDS = 16
ATOMS = 512
N_BAND = 16
N_SLAB = 8


def draw_orbitals(key, part):
    key = jax.random.fold_in(key, 11)
    full_shape = (BANDS, NG, NG, NG)
    key_rough = jax.random.fold_in(key, 0)
    key_phase = jax.random.fold_in(key, 2)
    key_turn = jax.random.fold_in(key, 3)
    noise = jax.random.truncated_normal(key_rough, -4.0, 4.0, full_shape, jnp.float32)
    banded = (jnp.roll(noise, -1, axis=1) - jnp.roll(noise, 1, axis=1)) * 0.70710678
    envelope = 1.0 + 0.3 * banded
    phase = jax.random.uniform(key_phase, (BANDS, 1, 1, 1), jnp.float32, -3.14159, 3.14159)
    turn = (2 * jax.random.randint(key_turn, (BANDS, 1, 1, 1), 0, 2) - 1).astype(jnp.int32)
    index = jnp.arange(NG, dtype=jnp.int32)
    quarter = (index[None, None, :, None] + turn * index[None, None, None, :]) % 4
    wave = 1.41421356 * jnp.cos(quarter.astype(jnp.float32) * (0.5 * math.pi) + phase)
    sign_x = (1 - 2 * (index % 2)).astype(jnp.float32)[None, :, None, None]
    odd_band = (jnp.arange(BANDS, dtype=jnp.int32) % 2)[:, None, None, None]
    pattern = jnp.where(odd_band == 1, wave * sign_x, 1.0)
    return (envelope * pattern).astype(jnp.bfloat16)


def draw_atom_home(key, part):
    key = jax.random.fold_in(key, 7)
    owners = N_BAND * N_SLAB
    capacity = (2 * ATOM_DEV + N_SLAB - 1) // N_SLAB
    slab_bricks = NG // N_SLAB // 2
    key_dense, key_slabs, key_x, key_y, key_z = jax.random.split(key, 5)
    dense_slab = jax.random.randint(key_dense, (), 0, N_SLAB).astype(jnp.int32)
    seats = (N_SLAB - 1) * capacity

    def owner_slabs(owner_key):
        key_seat, key_order = jax.random.split(owner_key)
        seat_index = jax.random.permutation(key_seat, seats)[:ATOM_DEV - capacity].astype(jnp.int32)
        others = (dense_slab + 1 + seat_index // capacity) % N_SLAB
        dense_part = jnp.zeros((capacity,), jnp.int32) + dense_slab
        return jax.random.permutation(key_order, jnp.concatenate([dense_part, others.astype(jnp.int32)]))
    slab_of = jax.vmap(owner_slabs)(jax.random.split(key_slabs, owners)).reshape(-1).astype(jnp.int32)
    along_x = slab_of * slab_bricks + jax.random.randint(key_x, (ATOMS,), 0, slab_bricks - 1)
    along_y = jax.random.randint(key_y, (ATOMS,), 0, NG // 8)
    along_z = jax.random.randint(key_z, (ATOMS,), 0, NG // 8)
    return jnp.stack([along_x, along_y, along_z]).astype(jnp.int32)


def level_of(key, extent, cuts, smallest, largest):
    level, own = 1.0, jax.random.fold_in(key, 6)
    for dim, blocks in cuts:
        steps = jnp.exp(jax.random.uniform(jax.random.fold_in(own, dim), (blocks,), jnp.float32, smallest / len(cuts), largest / len(cuts)))
        level = level * jnp.repeat(steps, extent[dim] // blocks).reshape([-1 if axis == dim else 1 for axis in range(len(extent))])
    return level


def normal_values(stream_key, dims, width, limit, shards=(), held_as=jnp.bfloat16):
    result = jax.random.normal(stream_key, dims, jnp.float32) * width
    if len(shards) > 0:
        result = level_of(stream_key, dims, shards, -0.22, 0.18) * result
    return jnp.clip(result, min=-limit, max=limit).astype(held_as)


def setup_inputs(seed: int = 0) -> dict:
    key_list = jax.random.split(jax.random.key(seed), 5)
    orbitals = draw_orbitals(jax.random.fold_in(key_list[4], 71), 0)
    projections = normal_values(key_list[1], (BANDS, NCH, ATOMS), 0.5, 4.0, ((0, 16),))
    aug_blocks = normal_values(key_list[2], (ATOMS, NBRK, NCH, BRICK), 0.5, 3.0, ((0, 128),))
    atom_home = draw_atom_home(jax.random.fold_in(key_list[4], 71), 0)
    return {"orbitals": orbitals, "projections": projections, "aug_blocks": aug_blocks, "atom_home": atom_home}


KERNEL_SCALE = 0.5
KERNEL_AT_ZERO = 0.0
SCREENING_RANGE = 0.002
HIGH = lax.Precision.HIGHEST


def fold_square(length):
    index = jnp.arange(length, dtype=jnp.int32)
    folded = jnp.minimum(index, length - index).astype(jnp.float32)
    return (folded * (2.0 * math.pi / length)) ** 2


def kernel_table():
    squares = fold_square(NG)
    summed_exchange = squares[:, None, None] + squares[None, :, None] + squares[None, None, :]
    return jnp.where(summed_exchange > 0, KERNEL_SCALE / (summed_exchange + SCREENING_RANGE), KERNEL_AT_ZERO).astype(jnp.float32)


def brick_positions(atom_home):
    bricks_side = NG // 8
    corner = jnp.arange(8, dtype=jnp.int32)
    along_x = atom_home[0][:, None] + corner[None, :] // 4
    along_y = (atom_home[1][:, None] + (corner[None, :] // 2) % 2) % bricks_side
    along_z = (atom_home[2][:, None] + corner[None, :] % 2) % bricks_side
    return ((along_x * bricks_side + along_y) * bricks_side + along_z).reshape(-1).astype(jnp.int32)


def place(kernel_values, placing):
    bricks_side = NG // 8
    flat = jnp.zeros(((NG // 2) * bricks_side * bricks_side, BRICK), jnp.float32)
    flat = flat.at[placing].add(kernel_values.reshape(-1, BRICK))
    shaped = flat.reshape(NG // 2, bricks_side, bricks_side, 2, 8, 8)
    return shaped.transpose(0, 3, 1, 4, 2, 5).reshape(NG, NG, NG)


def reference(orbitals, projections, aug_blocks, atom_home):
    coulomb_kernel = kernel_table()[:, :, : NG // 2 + 1]
    blocks = aug_blocks.astype(jnp.float32)
    project_all = projections.astype(jnp.float32)
    placing = brick_positions(atom_home)

    def one_band(i):
        group_of = i // NB
        orbital_i = lax.dynamic_index_in_dim(orbitals, i, 0, keepdims=False).astype(jnp.float32)
        project_i = lax.dynamic_index_in_dim(project_all, i, 0, keepdims=False)

        def add_partner(summed_exchange, t):
            j = (((group_of + t // NB - 1) % N_BAND) * NB + t % NB).astype(jnp.int32)
            orbital_j = lax.dynamic_index_in_dim(orbitals, j, 0, keepdims=False).astype(jnp.float32)
            project_j = lax.dynamic_index_in_dim(project_all, j, 0, keepdims=False)
            weights = project_i * project_j
            kernel_values = jnp.einsum("ca,akcn->akn", weights, blocks, precision=HIGH)
            density = orbital_i * orbital_j + place(kernel_values, placing)
            potential = jnp.fft.irfftn(jnp.fft.rfftn(density) * coulomb_kernel, s=(NG, NG, NG)).astype(jnp.float32)
            return summed_exchange + potential * orbital_j, None

        summed_exchange, _ = lax.scan(add_partner, jnp.zeros((NG, NG, NG), jnp.float32), jnp.arange(3 * NB, dtype=jnp.int32))
        return summed_exchange

    return lax.map(one_band, jnp.arange(NB * N_BAND, dtype=jnp.int32))
```

```python
import functools
import math

import numpy as np
import jax
import jax.numpy as jnp
from jax import lax
from jax.experimental import pallas as pl
from jax.experimental.pallas import tpu as pltpu
from jax.sharding import PartitionSpec as P

KERNEL_SCALE = 0.5
SCREENING_RANGE = 0.002
NG = 128
SLABS = 8
ROWS = NG // SLABS
PLANES = NG // SLABS
BLOCK_LIMIT = 3.0
QMAX = 32760.0
STEPS = 8.0
FWD_TILES = PLANES + 2
BACK_TILES = PLANES + 1
BF = jnp.bfloat16
F32 = jnp.float32
VMEM_LIMIT = 50 * 1024 * 1024


def hartley_host():
    index = np.arange(NG)
    angle = (index[:, None] * index[None, :] % NG) * (2.0 * math.pi / NG)
    return (np.cos(angle) + np.sin(angle)).astype(np.float32)


def split_host(table):
    high = table.astype(jnp.bfloat16)
    low = (table - high.astype(np.float32)).astype(jnp.bfloat16)
    return high, low


def row_order():
    by_size = sorted(range(NG), key=lambda k: (min(k, NG - k), k))
    return np.array([[by_size[d + SLABS * r] for r in range(ROWS)] for d in range(SLABS)])


def fold_square_host():
    index = np.arange(NG)
    return ((np.minimum(index, NG - index)).astype(np.float32) * np.float32(2.0 * math.pi / NG)) ** 2


def tables():
    table = hartley_host()
    high, low = split_host(table)
    order = row_order().reshape(-1)
    high_y, low_y = high[order], low[order]
    right = np.concatenate([high, high, low], axis=0)
    left = np.concatenate([high, low, high], axis=1)
    left_y = np.concatenate([high_y, low_y, high_y], axis=1)
    left_y_back = np.concatenate([high_y.T, low_y.T, high_y.T], axis=1)
    return right, left, left_y, left_y_back


def split(value):
    high = value.astype(BF)
    low = (value - high.astype(F32)).astype(BF)
    return high, low


def dot(a, b):
    return jnp.dot(a, b, preferred_element_type=F32)


def times_right(value, right_ref):
    high, low = split(value)
    both = jnp.concatenate([high, low], axis=1)
    return dot(both, right_ref[: 2 * NG, :]) + dot(high, right_ref[2 * NG :, :])


def times_left(left_ref, value):
    high, low = split(value)
    return dot(left_ref[...], jnp.concatenate([high, high, low], axis=0))


def step_code(largest):
    return jnp.ceil(jnp.log(jnp.maximum(largest, 1e-30)) * (STEPS / math.log(2.0)))


def step_size(code):
    return jnp.exp(code * (math.log(2.0) / STEPS)) * (1.001 / QMAX)


def to_int16(value):
    return value.astype(jnp.int32).astype(jnp.int16)


def from_int16(value):
    return value.astype(jnp.int32).astype(F32)


def charge_kernel(weight_ref, block_ref, out_ref, held):
    weight = weight_ref[...]
    bound = jnp.sum(jnp.abs(weight), axis=1, keepdims=True) * BLOCK_LIMIT
    factor = QMAX / jnp.maximum(bound, 1e-30)
    high, low = split(weight)
    both = jnp.concatenate([high, low], axis=0)
    rows = weight.shape[0]
    for y in range(8):
        product = dot(both, block_ref[y])
        held[:, y, :] = (product[:rows] + product[rows:]) * factor
    half = rows // 2
    both_pairs = jnp.concatenate([held[:half], held[half:]], axis=1)
    out_ref[...] = to_int16(jnp.round(both_pairs))


def density_kernel(home_ref, scale_ref, charge_ref, own_ref, next_ref, right_ref, left_ref, out_ref, field):
    for x in range(PLANES):
        own = own_ref[x].astype(F32)
        field[0, x] = own * own
        field[1, x] = own * next_ref[x].astype(F32)
    lane = lax.broadcasted_iota(jnp.int32, (8, NG), 1)

    def add_atom(d, carry):
        plane = home_ref[0, d]
        brick_y = home_ref[1, d]
        shift = home_ref[2, d] * 8
        values = from_int16(charge_ref[d])
        inside = ((lane - shift) & (NG - 1)) < 16
        places = []
        for p in range(2):
            tile = values[8 * p : 8 * p + 8] * scale_ref[p, d]
            for g in range(8):
                turned = pltpu.roll(tile, (shift + (NG - 16 * g)) & (NG - 1), 1)
                row = pl.multiple_of(((brick_y + g % 2) & (NG // 8 - 1)) * 8, 8)
                at = (p, plane + g // 2, pl.ds(row, 8))
                places.append((at, field[at] + jnp.where(inside, turned, 0.0)))
        for at, total in places:
            field[at] = total
        return carry

    lax.fori_loop(0, charge_ref.shape[0], add_atom, 0)

    def transform(p, carry):
        for x in range(0, PLANES, 2):
            first = times_right(field[p, x], right_ref)
            second = times_right(field[p, x + 1], right_ref)
            both = times_left(left_ref, jnp.concatenate([first, second], axis=1))
            field[p, x] = both[:, :NG]
            field[p, x + 1] = both[:, NG:]
        return carry

    lax.fori_loop(0, 2, transform, 0)

    def pack(n, carry):
        p = n // SLABS
        d = n % SLABS
        rows = pl.ds(pl.multiple_of(d * ROWS, ROWS), ROWS)
        largest = jnp.abs(field[p, 0, rows])
        for x in range(1, PLANES):
            largest = jnp.maximum(largest, jnp.abs(field[p, x, rows]))
        code = step_code(largest)
        factor = 1.0 / step_size(code)
        base = p * FWD_TILES
        lows = []
        for x in range(PLANES):
            scaled = field[p, x, rows] * factor
            whole = jnp.round(scaled)
            out_ref[d, base + x] = to_int16(whole)
            lows.append((scaled - whole)[0:1])
        out_ref[d, base + PLANES] = to_int16(code)
        low = jnp.concatenate(lows, axis=0) * (2.0 * QMAX)
        out_ref[d, base + PLANES + 1] = to_int16(jnp.round(low))
        return carry

    lax.fori_loop(0, 2 * SLABS, pack, 0)


def solve_kernel(square_ref, in_ref, fold_x_ref, fold_z_ref, left_ref, out_ref, field):
    def unpack(n, carry):
        p = n // SLABS
        s = n % SLABS
        base = p * FWD_TILES
        step = step_size(from_int16(in_ref[s, base + PLANES]))
        for x in range(PLANES):
            field[p, s * PLANES + x] = from_int16(in_ref[s, base + x]) * step
        low = from_int16(in_ref[s, base + PLANES + 1]) * (step[0:1] * (0.5 / QMAX))
        planes = pl.ds(s * PLANES, PLANES)
        field[p, planes, 0, :] = field[p, planes, 0, :] + low
        return carry

    lax.fori_loop(0, 2 * SLABS, unpack, 0)
    fold = fold_x_ref[...] + fold_z_ref[...]
    for r in range(ROWS):
        total = fold + square_ref[r]
        table = jnp.where(total > 0, KERNEL_SCALE / (total + SCREENING_RANGE), 0.0) * (1.0 / NG**3)
        columns = jnp.concatenate([field[0, :, r, :], field[1, :, r, :]], axis=1)
        spectrum = times_left(left_ref, columns)
        spectrum = spectrum * jnp.concatenate([table, table], axis=1)
        columns = times_left(left_ref, spectrum)
        field[0, :, r, :] = columns[:, :NG]
        field[1, :, r, :] = columns[:, NG:]

    def pack(n, carry):
        p = n // SLABS
        s = n % SLABS
        base = p * BACK_TILES
        largest = jnp.abs(field[p, s * PLANES])
        for x in range(1, PLANES):
            largest = jnp.maximum(largest, jnp.abs(field[p, s * PLANES + x]))
        code = step_code(largest)
        factor = 1.0 / step_size(code)
        for x in range(PLANES):
            out_ref[s, base + x] = to_int16(jnp.round(field[p, s * PLANES + x] * factor))
        out_ref[s, base + PLANES] = to_int16(code)
        return carry

    lax.fori_loop(0, 2 * SLABS, pack, 0)


def potential_pair(in_ref, steps, x, p, left_ref, right_ref):
    base = p * BACK_TILES + x
    halves = []
    for k in range(2):
        halves.append(jnp.concatenate([from_int16(in_ref[s, base + k]) * steps[s] for s in range(SLABS)], axis=0))
    both = times_left(left_ref, jnp.concatenate(halves, axis=1))
    return times_right(both[:, :NG], right_ref), times_right(both[:, NG:], right_ref)


def back_cross_kernel(in_ref, own_ref, next_ref, left_ref, right_ref, kept_ref, sent_ref, codes):
    steps = [step_size(from_int16(in_ref[s, BACK_TILES + PLANES])) for s in range(SLABS)]
    for x in range(0, PLANES, 2):
        pair = potential_pair(in_ref, steps, x, 1, left_ref, right_ref)
        for k in range(2):
            potential = pair[k]
            kept_ref[x + k] = potential * next_ref[x + k].astype(F32)
            product = potential * own_ref[x + k].astype(F32)
            code = step_code(jnp.max(jnp.abs(product), axis=0, keepdims=True))
            codes[x + k : x + k + 1, :] = code
            sent_ref[pl.ds((x + k) * NG, NG), :] = to_int16(jnp.round(product * (1.0 / step_size(code))))
    sent_ref[pl.ds(PLANES * NG, PLANES), :] = to_int16(codes[...])


def back_own_kernel(in_ref, own_ref, kept_ref, left_ref, right_ref, out_ref):
    steps = [step_size(from_int16(in_ref[s, PLANES])) for s in range(SLABS)]
    for x in range(0, PLANES, 2):
        pair = potential_pair(in_ref, steps, x, 0, left_ref, right_ref)
        for k in range(2):
            out_ref[x + k] = kept_ref[x + k] + pair[k] * own_ref[x + k].astype(F32)


def add_kernel(sum_ref, sent_ref, out_ref):
    steps = step_size(from_int16(sent_ref[pl.ds(PLANES * NG, PLANES), :]))
    for x in range(PLANES):
        out_ref[0, x] = sum_ref[x] + from_int16(sent_ref[pl.ds(x * NG, NG), :]) * steps[x : x + 1]


def vmem():
    return pl.BlockSpec(memory_space=pltpu.VMEM)


def smem():
    return pl.BlockSpec(memory_space=pltpu.SMEM)


def call(kernel, in_specs, out_shape, scratch, name):
    many = isinstance(out_shape, (list, tuple))
    return pl.pallas_call(
        kernel,
        in_specs=in_specs,
        out_specs=[vmem() for _ in out_shape] if many else vmem(),
        out_shape=out_shape,
        scratch_shapes=scratch,
        name=name,
        compiler_params=pltpu.CompilerParams(vmem_limit_bytes=VMEM_LIMIT),
    )


def from_behind(block, axis, distance):
    count = lax.axis_size(axis)
    return lax.ppermute(block, axis, [((i - distance) % count, i) for i in range(count)])


def per_device(orbitals, projections, aug_blocks, atom_home):
    n_band = lax.axis_size("band")
    n_slab = lax.axis_size("slab")
    owners = n_band * n_slab
    atom_dev = aug_blocks.shape[0]
    channels = projections.shape[1]
    slab_bricks = PLANES // 2
    my_slab = lax.axis_index("slab")
    owner_me = lax.axis_index("band") * n_slab + my_slab
    right, left, left_y, left_y_back = (jnp.asarray(t) for t in tables())
    squares = fold_square_host()
    fold_rows = jnp.asarray(squares[row_order()])

    own = orbitals[0]
    own_proj = projections[0]
    next_proj = from_behind(own_proj, "band", -1)
    nxt = from_behind(own, "band", -1)

    by_owner = own_proj.reshape(channels, n_band, n_slab, atom_dev)
    mine = lax.dynamic_index_in_dim(by_owner, my_slab, 2, keepdims=False)
    mine = mine.transpose(1, 2, 0).reshape(n_band, atom_dev * channels)
    all_proj = lax.all_to_all(mine, "band", split_axis=0, concat_axis=0, tiled=True).astype(F32)

    slab_of = (atom_home[0] // slab_bricks).reshape(owners, atom_dev)
    here = slab_of == my_slab
    home = atom_home.reshape(3, owners, atom_dev)
    home = home - jnp.array([1, 0, 0], jnp.int32)[:, None, None] * (my_slab * slab_bricks)
    home = jnp.sum(jnp.where(here[None], home, 0), axis=2) * jnp.array([2, 1, 1], jnp.int32)[:, None]

    my_slabs = lax.dynamic_index_in_dim(slab_of, owner_me, 0, keepdims=False)
    goes = (my_slabs[None, :] == jnp.arange(n_slab, dtype=jnp.int32)[:, None]).astype(F32)
    goes = jnp.repeat(goes, channels, axis=1)
    pairs = jnp.stack([all_proj * all_proj, all_proj * jnp.roll(all_proj, -1, axis=0)])
    weight = (pairs[:, :, None, :] * goes[None, None]).reshape(2 * owners, atom_dev * channels)
    blocks = aug_blocks.reshape(atom_dev, 2, 2, 2, channels, 2, 8, 8)
    blocks = blocks.transpose(6, 0, 4, 1, 5, 2, 3, 7).reshape(8, atom_dev * channels, NG)
    charges = call(
        charge_kernel,
        [vmem(), vmem()],
        jax.ShapeDtypeStruct((owners, 16, NG), jnp.int16),
        [pltpu.VMEM((2 * owners, 8, NG), F32)],
        "charges",
    )(weight, blocks)
    charges = lax.all_to_all(charges, ("band", "slab"), split_axis=0, concat_axis=0, tiled=True)

    own_wide = own_proj.astype(F32)
    bound = jnp.stack([own_wide * own_wide, own_wide * next_proj.astype(F32)])
    bound = jnp.sum(jnp.abs(bound), axis=1).reshape(2, owners, atom_dev)
    bound = jnp.sum(jnp.where(here[None], bound, 0.0), axis=2) * (BLOCK_LIMIT / QMAX)

    spectrum = call(
        density_kernel,
        [smem(), smem()] + [vmem()] * 5,
        jax.ShapeDtypeStruct((n_slab, 2 * FWD_TILES, 16, NG), jnp.int16),
        [pltpu.VMEM((2, PLANES, NG, NG), F32)],
        "density",
    )(home, bound, charges, own, nxt, right, left_y)
    spectrum = lax.all_to_all(spectrum, "slab", split_axis=0, concat_axis=0, tiled=True)

    columns = call(
        solve_kernel,
        [smem()] + [vmem()] * 4,
        jax.ShapeDtypeStruct((n_slab, 2 * BACK_TILES, 16, NG), jnp.int16),
        [pltpu.VMEM((2, NG, ROWS, NG), F32)],
        "solve",
    )(
        lax.dynamic_index_in_dim(fold_rows, my_slab, 0, keepdims=False),
        spectrum,
        jnp.asarray(np.broadcast_to(squares[:, None], (NG, NG)).copy()),
        jnp.asarray(squares[None, :]),
        left,
    )
    columns = lax.all_to_all(columns, "slab", split_axis=0, concat_axis=0, tiled=True)

    kept, sent = call(
        back_cross_kernel,
        [vmem()] * 5,
        [
            jax.ShapeDtypeStruct((PLANES, NG, NG), F32),
            jax.ShapeDtypeStruct((PLANES * NG + PLANES, NG), jnp.int16),
        ],
        [pltpu.VMEM((PLANES, NG), F32)],
        "back_cross",
    )(columns, own, nxt, left_y_back, right)
    got = from_behind(sent, "band", 1)
    total = call(
        back_own_kernel,
        [vmem()] * 5,
        jax.ShapeDtypeStruct((PLANES, NG, NG), F32),
        [],
        "back_own",
    )(columns, own, kept, left_y_back, right)
    return call(
        add_kernel,
        [vmem()] * 2,
        jax.ShapeDtypeStruct((1, PLANES, NG, NG), F32),
        [],
        "add_previous",
    )(total, got)


def solution(mesh):
    in_specs = (
        P("band", "slab", None, None),
        P("band", None, None),
        P(("band", "slab"), None, None, None),
        P(),
    )
    out_specs = P("band", "slab", None, None)
    return jax.shard_map(
        per_device, mesh=mesh, in_specs=in_specs, out_specs=out_specs, check_vma=False
    )
```

```python
import functools
import math

import numpy as np
import jax
import jax.numpy as jnp
from jax import lax
from jax.experimental import pallas as pl
from jax.experimental.pallas import tpu as pltpu
from jax.sharding import PartitionSpec as P

KERNEL_SCALE = 0.5
SCREENING_RANGE = 0.002
NG = 128
SLABS = 8
ROWS = NG // SLABS
PLANES = NG // SLABS
BLOCK_LIMIT = 3.0
QMAX = 32760.0
STEPS = 8.0
CHANNELS = 9
CHANNEL_ROWS = 16
FWD_TILES = PLANES + 2
BACK_TILES = PLANES + 1
BF = jnp.bfloat16
F32 = jnp.float32
VMEM_LIMIT = 50 * 1024 * 1024


def hartley_host():
    index = np.arange(NG)
    angle = (index[:, None] * index[None, :] % NG) * (2.0 * math.pi / NG)
    return (np.cos(angle) + np.sin(angle)).astype(np.float32)


def split_host(table):
    high = table.astype(jnp.bfloat16)
    low = (table - high.astype(np.float32)).astype(jnp.bfloat16)
    return high, low


def row_order():
    by_size = sorted(range(NG), key=lambda k: (min(k, NG - k), k))
    return np.array([[by_size[d + SLABS * r] for r in range(ROWS)] for d in range(SLABS)])


def fold_square_host():
    index = np.arange(NG)
    return ((np.minimum(index, NG - index)).astype(np.float32) * np.float32(2.0 * math.pi / NG)) ** 2


def tables():
    table = hartley_host()
    high, low = split_host(table)
    order = row_order().reshape(-1)
    high_y, low_y = high[order], low[order]
    top = np.concatenate([high, low], axis=1)
    bottom = np.concatenate([high, np.zeros_like(high)], axis=1)
    right = np.concatenate([top, bottom], axis=0)
    left = np.concatenate([high, low, high], axis=1)
    left_y = np.concatenate([high_y, low_y, high_y], axis=1)
    left_y_back = np.concatenate([high_y.T, low_y.T, high_y.T], axis=1)
    return right, left, left_y, left_y_back


def split(value):
    high = value.astype(BF)
    low = (value - high.astype(F32)).astype(BF)
    return high, low


def dot(a, b):
    return jnp.dot(a, b, preferred_element_type=F32)


def times_right(value, right_ref):
    high, low = split(value)
    both = dot(jnp.concatenate([high, low], axis=1), right_ref[...])
    return both[:, :NG] + both[:, NG:]


def times_left(left_ref, value):
    high, low = split(value)
    return dot(left_ref[...], jnp.concatenate([high, high, low], axis=0))


def step_code(largest):
    return jnp.ceil(jnp.log(jnp.maximum(largest, 1e-30)) * (STEPS / math.log(2.0)))


def step_size(code):
    return jnp.exp(code * (math.log(2.0) / STEPS)) * (1.001 / QMAX)


def to_int16(value):
    return value.astype(jnp.int32).astype(jnp.int16)


def from_int16(value):
    return value.astype(jnp.int32).astype(F32)


def block_kernel(block_ref, out_ref, rows, turned):
    lane = lax.broadcasted_iota(jnp.int32, (1, NG), 1) // 8
    atoms, bricks, channels = block_ref.shape[:3]
    rows[...] = jnp.zeros_like(rows)
    for k in range(bricks):
        for t in range(atoms):
            rows[k, pl.ds(CHANNEL_ROWS * t, channels), :] = block_ref[t, k].astype(F32)
    for k in range(bricks):
        values = rows[k]
        first = (k // 4) * 8 + (k // 2 % 2) * 2 + k % 2
        for back in range(12):
            moved = pltpu.roll(values, (first - back) % 16 * 8, 1)
            for x in range(2):
                y = back - 4 * x
                if 0 <= y < 8:
                    inside = lane == first + 4 * x
                    turned[y] = moved if k == 0 and x == 0 else jnp.where(inside, moved, turned[y])
    out_ref[...] = turned[...].astype(BF)


def message_kernel(proj_ref, out_ref, rows):
    rows[...] = jnp.zeros_like(rows)
    rows[pl.ds(0, proj_ref.shape[1]), :] = proj_ref[0].astype(F32)
    total = rows.shape[1]
    count = out_ref.shape[0]
    for b in range(count):
        moved = pltpu.roll(rows[...], (total - b * (total // count)) % total, 1)
        out_ref[b] = moved[:, :NG].astype(BF)


def charge_kernel(home_ref, proj_ref, block_ref, out_ref, held):
    slab = lax.axis_index("slab")
    owner = lax.axis_index("band") * SLABS + slab
    groups = proj_ref.shape[0]
    atoms = block_ref.shape[1] // CHANNEL_ROWS
    lane = lax.broadcasted_iota(jnp.int32, (CHANNEL_ROWS, NG), 1)
    weights = [jnp.zeros((CHANNEL_ROWS, NG), F32)] * atoms
    for b in range(groups):
        mine = pltpu.roll(proj_ref[b].astype(F32), (NG - slab * atoms) & (NG - 1), 1)
        for t in range(atoms):
            weights[t] = jnp.where(lane // SLABS == b, mine[:, t : t + 1], weights[t])
    pieces = []
    for t in range(atoms):
        goes = (lane & (SLABS - 1)) == home_ref[0, owner * atoms + t] // (PLANES // 2)
        behind = pltpu.roll(weights[t], NG - SLABS, 1)
        pairs = [jnp.where(goes, weights[t] * other, 0.0) for other in (weights[t], behind)]
        pieces.append(jnp.concatenate(pairs, axis=1))
    weight = jnp.concatenate(pieces, axis=0)
    bound = jnp.sum(jnp.abs(weight), axis=0, keepdims=True) * BLOCK_LIMIT
    weight = jnp.transpose(weight * (QMAX / jnp.maximum(bound, 1e-30)))
    both = jnp.concatenate(split(weight), axis=1)
    for y in range(8):
        held[:, y, :] = dot(both, jnp.concatenate([block_ref[y], block_ref[y]], axis=0))
    half = weight.shape[0] // 2
    both_pairs = jnp.concatenate([held[:half], held[half:]], axis=1)
    out_ref[...] = to_int16(jnp.round(both_pairs))


def mark_kernel(in_ref, out_ref):
    out_ref[...] = jnp.zeros_like(out_ref)


def density_kernel(p, home_ref, here_ref, charge_ref, own_ref, next_ref, right_ref, left_ref, out_ref, field, scales):
    rows, owners = here_ref.shape[0], charge_ref.shape[0]
    proj = pl.ds(PLANES * NG, own_ref.shape[0] - PLANES * NG)
    sizes = jnp.abs(own_ref[proj, :].astype(F32) * next_ref[proj, :].astype(F32))
    bound = sizes[:rows]
    for c in range(1, CHANNELS):
        bound = bound + sizes[c * rows : (c + 1) * rows]
    bound = bound * here_ref[...] * (BLOCK_LIMIT / QMAX)
    count = owners // rows
    wide = lax.broadcasted_iota(jnp.int32, (count, NG), 1) // (NG // count)
    own_lane = wide == lax.broadcasted_iota(jnp.int32, (count, NG), 0)
    for r in range(rows):
        picked = jnp.where(own_lane, bound[r : r + 1], 0.0)
        total = jnp.sum(picked, axis=1, keepdims=True)
        scales[pl.ds(r * count, count), :] = jnp.broadcast_to(total, (count, NG))
    for x in range(PLANES):
        plane = pl.ds(x * NG, NG)
        field[x] = own_ref[plane, :].astype(F32) * next_ref[plane, :].astype(F32)
    lane = lax.broadcasted_iota(jnp.int32, (8, NG), 1)

    def add_atom(d, carry):
        plane = home_ref[0, d]
        brick_y = home_ref[1, d]
        shift = home_ref[2, d] * 8
        inside = ((lane - shift) & (NG - 1)) < 16
        places = []
        tile = from_int16(charge_ref[d])[8 * p : 8 * p + 8] * scales[pl.ds(d, 1), :]
        for g in range(8):
            turned = pltpu.roll(tile, (shift + (NG - 16 * g)) & (NG - 1), 1)
            row = pl.multiple_of(((brick_y + g % 2) & (NG // 8 - 1)) * 8, 8)
            at = (plane + g // 2, pl.ds(row, 8))
            places.append((at, field[at] + jnp.where(inside, turned, 0.0)))
        for at, total in places:
            field[at] = total
        return carry

    lax.fori_loop(0, charge_ref.shape[0], add_atom, 0, unroll=32)
    for x in range(0, PLANES, 2):
        both = times_right(jnp.concatenate([field[x], field[x + 1]], axis=0), right_ref)
        both = times_left(left_ref, jnp.concatenate([both[:NG], both[NG:]], axis=1))
        field[x] = both[:, :NG]
        field[x + 1] = both[:, NG:]

    def pack(d, carry):
        rows = pl.ds(pl.multiple_of(d * ROWS, ROWS), ROWS)
        largest = jnp.abs(field[0, rows])
        for x in range(1, PLANES):
            largest = jnp.maximum(largest, jnp.abs(field[x, rows]))
        code = step_code(largest)
        factor = 1.0 / step_size(code)
        lows = []
        for x in range(PLANES):
            scaled = field[x, rows] * factor
            whole = jnp.round(scaled)
            out_ref[d, x] = to_int16(whole)
            lows.append((scaled - whole)[0:1])
        out_ref[d, PLANES] = to_int16(code)
        low = jnp.concatenate(lows, axis=0) * (2.0 * QMAX)
        out_ref[d, PLANES + 1] = to_int16(jnp.round(low))
        return carry

    lax.fori_loop(0, SLABS, pack, 0, unroll=True)


def solve_kernel(square_ref, in_ref, fold_x_ref, fold_z_ref, left_ref, out_ref, field):
    def unpack(s, carry):
        step = step_size(from_int16(in_ref[s, PLANES]))
        for x in range(PLANES):
            field[s * PLANES + x] = from_int16(in_ref[s, x]) * step
        low = from_int16(in_ref[s, PLANES + 1]) * (step[0:1] * (0.5 / QMAX))
        planes = pl.ds(s * PLANES, PLANES)
        field[planes, 0, :] = field[planes, 0, :] + low
        return carry

    lax.fori_loop(0, SLABS, unpack, 0, unroll=True)
    fold = fold_x_ref[...] + fold_z_ref[...]
    for r in range(0, ROWS, 2):
        halves = []
        for k in range(2):
            total = fold + square_ref[r + k]
            halves.append(jnp.where(total > 0, KERNEL_SCALE / (total + SCREENING_RANGE), 0.0) * (1.0 / NG**3))
        columns = jnp.concatenate([field[:, r, :], field[:, r + 1, :]], axis=1)
        spectrum = times_left(left_ref, columns) * jnp.concatenate(halves, axis=1)
        columns = times_left(left_ref, spectrum)
        field[:, r, :] = columns[:, :NG]
        field[:, r + 1, :] = columns[:, NG:]

    def pack(s, carry):
        largest = jnp.abs(field[s * PLANES])
        for x in range(1, PLANES):
            largest = jnp.maximum(largest, jnp.abs(field[s * PLANES + x]))
        code = step_code(largest)
        factor = 1.0 / step_size(code)
        for x in range(PLANES):
            out_ref[s, x] = to_int16(jnp.round(field[s * PLANES + x] * factor))
        out_ref[s, PLANES] = to_int16(code)
        return carry

    lax.fori_loop(0, SLABS, pack, 0, unroll=True)


def potential_pair(in_ref, steps, x, left_ref, right_ref):
    halves = []
    for k in range(2):
        halves.append(jnp.concatenate([from_int16(in_ref[s, x + k]) * steps[s] for s in range(SLABS)], axis=0))
    both = times_left(left_ref, jnp.concatenate(halves, axis=1))
    both = times_right(jnp.concatenate([both[:, :NG], both[:, NG:]], axis=0), right_ref)
    return both[:NG], both[NG:]


def back_cross_kernel(in_ref, own_ref, next_ref, left_ref, right_ref, kept_ref, sent_ref, codes):
    steps = [step_size(from_int16(in_ref[s, PLANES])) for s in range(SLABS)]
    for x in range(0, PLANES, 2):
        pair = potential_pair(in_ref, steps, x, left_ref, right_ref)
        for k in range(2):
            potential = pair[k]
            kept_ref[x + k] = potential * next_ref[pl.ds((x + k) * NG, NG), :].astype(F32)
            product = potential * own_ref[pl.ds((x + k) * NG, NG), :].astype(F32)
            code = step_code(jnp.max(jnp.abs(product), axis=0, keepdims=True))
            codes[x + k : x + k + 1, :] = code
            sent_ref[pl.ds((x + k) * NG, NG), :] = to_int16(jnp.round(product * (1.0 / step_size(code))))
    sent_ref[pl.ds(PLANES * NG, PLANES), :] = to_int16(codes[...])


def back_own_kernel(in_ref, own_ref, kept_ref, sent_ref, left_ref, right_ref, out_ref):
    steps = [step_size(from_int16(in_ref[s, PLANES])) for s in range(SLABS)]
    sent_steps = step_size(from_int16(sent_ref[pl.ds(PLANES * NG, PLANES), :]))
    for x in range(0, PLANES, 2):
        pair = potential_pair(in_ref, steps, x, left_ref, right_ref)
        for k in range(2):
            sent = from_int16(sent_ref[pl.ds((x + k) * NG, NG), :]) * sent_steps[x + k : x + k + 1]
            out_ref[0, x + k] = kept_ref[x + k] + sent + pair[k] * own_ref[pl.ds((x + k) * NG, NG), :].astype(F32)


def vmem():
    return pl.BlockSpec(memory_space=pltpu.VMEM)


def smem():
    return pl.BlockSpec(memory_space=pltpu.SMEM)


def call(kernel, in_specs, out_shape, scratch, name, micros):
    many = isinstance(out_shape, (list, tuple))
    return pl.pallas_call(
        kernel,
        in_specs=in_specs,
        out_specs=[vmem() for _ in out_shape] if many else vmem(),
        out_shape=out_shape,
        scratch_shapes=scratch,
        name=name,
        cost_estimate=pl.CostEstimate(
            flops=int(micros * 1e8), bytes_accessed=int(micros * 3.5e6), transcendentals=0
        ),
        compiler_params=pltpu.CompilerParams(vmem_limit_bytes=VMEM_LIMIT),
    )


def mark(array):
    whole = [pl.BlockSpec(memory_space=pl.ANY)]
    return call(mark_kernel, whole, jax.ShapeDtypeStruct((8, NG), F32), [], "mark", 30)(array)


def from_behind(block, axis, distance):
    count = lax.axis_size(axis)
    return lax.ppermute(block, axis, [((i - distance) % count, i) for i in range(count)])


def per_device(orbitals, projections, aug_blocks, atom_home):
    n_band = lax.axis_size("band")
    n_slab = lax.axis_size("slab")
    owners = n_band * n_slab
    atom_dev = aug_blocks.shape[0]
    channels = projections.shape[1]
    slab_bricks = PLANES // 2
    my_slab = lax.axis_index("slab")
    right, left, left_y, left_y_back = (jnp.asarray(t) for t in tables())
    squares = fold_square_host()
    fold_rows = jnp.asarray(squares[row_order()])

    own = orbitals[0]
    own_proj = projections[0]

    messages = call(
        message_kernel,
        [vmem()],
        jax.ShapeDtypeStruct((n_band, CHANNEL_ROWS, NG), BF),
        [pltpu.VMEM((CHANNEL_ROWS, projections.shape[2]), F32)],
        "messages",
        1,
    )(projections)
    messages, late_blocks = lax.optimization_barrier((messages, aug_blocks))
    all_proj = lax.all_to_all(messages, "band", split_axis=0, concat_axis=0, tiled=True)

    slab_of = (atom_home[0] // slab_bricks).reshape(owners, atom_dev)
    here = slab_of == my_slab
    home = atom_home.reshape(3, owners, atom_dev)
    home = home - jnp.array([1, 0, 0], jnp.int32)[:, None, None] * (my_slab * slab_bricks)
    home = jnp.sum(jnp.where(here[None], home, 0), axis=2) * jnp.array([2, 1, 1], jnp.int32)[:, None]

    blocks = call(
        block_kernel,
        [vmem()],
        jax.ShapeDtypeStruct((8, atom_dev * CHANNEL_ROWS, NG), BF),
        [pltpu.VMEM((8, atom_dev * CHANNEL_ROWS, NG), F32)] * 2,
        "blocks",
        1,
    )(late_blocks)
    wide_proj = own_proj.reshape(-1, NG)
    fill = jnp.zeros((-wide_proj.shape[0] % 16, NG), BF)
    both = jnp.concatenate([own.reshape(-1, NG), wide_proj, fill], axis=0)
    here = here.astype(F32).reshape(-1, NG)
    both, home, here, blocks = lax.optimization_barrier((both, home, here, blocks))
    nxt = from_behind(both, "band", -1)

    charges = call(
        charge_kernel,
        [smem()] + [vmem()] * 2,
        jax.ShapeDtypeStruct((owners, 16, NG), jnp.int16),
        [pltpu.VMEM((2 * owners, 8, NG), F32)],
        "charges",
        2,
    )(atom_home, all_proj, blocks)
    charges = lax.all_to_all(charges, ("band", "slab"), split_axis=0, concat_axis=0, tiled=True)

    fold_y = lax.dynamic_index_in_dim(fold_rows, my_slab, 0, keepdims=False)
    fold_x = jnp.asarray(np.broadcast_to(squares[:, None], (NG, NG)).copy())
    fold_z = jnp.asarray(squares[None, :])

    def density(p, other):
        return call(
            functools.partial(density_kernel, p),
            [smem()] + [vmem()] * 6,
            jax.ShapeDtypeStruct((n_slab, FWD_TILES, 16, NG), jnp.int16),
            [pltpu.VMEM((PLANES, NG, NG), F32), pltpu.VMEM((owners, NG), F32)],
            "density" + str(p),
            6,
        )(home, here, charges, both, other, right, left_y)

    def solve(p, spectrum):
        return call(
            solve_kernel,
            [smem()] + [vmem()] * 4,
            jax.ShapeDtypeStruct((n_slab, BACK_TILES, 16, NG), jnp.int16),
            [pltpu.VMEM((NG, ROWS, NG), F32)],
            "solve" + str(p),
            3,
        )(fold_y, spectrum, fold_x, fold_z, left)

    def swap(block):
        return lax.all_to_all(block, "slab", split_axis=0, concat_axis=0, tiled=True)

    cross = swap(density(1, nxt))
    mine = density(0, both)
    cross, mine = lax.optimization_barrier((cross, mine))
    mine = swap(mine)
    cross = solve(1, cross)
    cross, mine = lax.optimization_barrier((cross, mine))
    cross = swap(cross)
    mine = solve(0, mine)
    cross, mine = lax.optimization_barrier((cross, mine))
    mine = swap(mine)

    kept, sent = call(
        back_cross_kernel,
        [vmem()] * 5,
        [
            jax.ShapeDtypeStruct((PLANES, NG, NG), F32),
            jax.ShapeDtypeStruct((PLANES * NG + PLANES, NG), jnp.int16),
        ],
        [pltpu.VMEM((PLANES, NG), F32)],
        "back_cross",
        2,
    )(cross, both, nxt, left_y_back, right)
    got = from_behind(sent, "band", 1)
    got, _ = lax.optimization_barrier((got, mark(mine)))
    return call(
        back_own_kernel,
        [vmem()] * 6,
        jax.ShapeDtypeStruct((1, PLANES, NG, NG), F32),
        [],
        "back_own",
        2,
    )(mine, both, kept, got, left_y_back, right)


def solution(mesh):
    in_specs = (
        P("band", "slab", None, None),
        P("band", None, None),
        P(("band", "slab"), None, None, None),
        P(),
    )
    out_specs = P("band", "slab", None, None)
    return jax.shard_map(
        per_device, mesh=mesh, in_specs=in_specs, out_specs=out_specs, check_vma=False
    )
```

```python
import functools
import math

import numpy as np
import jax
import jax.numpy as jnp
from jax import lax
from jax.experimental import pallas as pl
from jax.experimental.pallas import tpu as pltpu
from jax.sharding import PartitionSpec as P

KERNEL_SCALE = 0.5
SCREENING_RANGE = 0.002
NG = 128
SLABS = 8
ROWS = NG // SLABS
PLANES = NG // SLABS
BLOCK_LIMIT = 3.0
QMAX = 32760.0
STEPS = 8.0
CHANNEL_ROWS = 16
FWD_TILES = PLANES + 2
BACK_TILES = PLANES + 1
BF = jnp.bfloat16
F32 = jnp.float32
VMEM_LIMIT = 50 * 1024 * 1024


def hartley_host():
    index = np.arange(NG)
    angle = (index[:, None] * index[None, :] % NG) * (2.0 * math.pi / NG)
    return (np.cos(angle) + np.sin(angle)).astype(np.float32)


def split_host(table):
    high = table.astype(jnp.bfloat16)
    low = (table - high.astype(np.float32)).astype(jnp.bfloat16)
    return high, low


def row_order():
    by_size = sorted(range(NG), key=lambda k: (min(k, NG - k), k))
    return np.array([[by_size[d + SLABS * r] for r in range(ROWS)] for d in range(SLABS)])


def fold_square_host():
    index = np.arange(NG)
    return ((np.minimum(index, NG - index)).astype(np.float32) * np.float32(2.0 * math.pi / NG)) ** 2


def tables():
    table = hartley_host()
    high, low = split_host(table)
    order = row_order().reshape(-1)
    high_y, low_y = high[order], low[order]
    top = np.concatenate([high, low], axis=1)
    bottom = np.concatenate([high, np.zeros_like(high)], axis=1)
    right = np.concatenate([top, bottom], axis=0)
    left = np.concatenate([high, low, high], axis=1)
    left_y = np.concatenate([high_y, low_y, high_y], axis=1)
    left_y_back = np.concatenate([high_y.T, low_y.T, high_y.T], axis=1)
    return right, left, left_y, left_y_back


def split(value):
    high = value.astype(BF)
    low = (value - high.astype(F32)).astype(BF)
    return high, low


def dot(a, b):
    return jnp.dot(a, b, preferred_element_type=F32)


def times_right(value, right_ref):
    high, low = split(value)
    both = dot(jnp.concatenate([high, low], axis=1), right_ref[...])
    return both[:, :NG] + both[:, NG:]


def times_left(left_ref, value):
    high, low = split(value)
    return dot(left_ref[...], jnp.concatenate([high, high, low], axis=0))


def step_code(largest):
    return jnp.ceil(jnp.log(jnp.maximum(largest, 1e-30)) * (STEPS / math.log(2.0)))


def step_size(code):
    return jnp.exp(code * (math.log(2.0) / STEPS)) * (1.001 / QMAX)


def to_int16(value):
    return value.astype(jnp.int32).astype(jnp.int16)


def from_int16(value):
    return value.astype(jnp.int32).astype(F32)


def local_kernel(after_ref, home_any, block_ref, out_ref, place_ref, here_ref, rows, turned, home_ref, sem):
    fetch = pltpu.make_async_copy(home_any, home_ref, sem)
    fetch.start()
    lane = lax.broadcasted_iota(jnp.int32, (1, NG), 1) // 8
    atoms, channels, bricks = block_ref.shape[:3]
    rows[...] = jnp.zeros_like(rows)
    for t in range(atoms):
        rows[:, pl.ds(CHANNEL_ROWS * t, channels), :] = jnp.swapaxes(block_ref[t].astype(F32), 0, 1)
    for k in range(bricks):
        values = rows[k]
        first = (k // 4) * 8 + (k // 2 % 2) * 2 + k % 2
        for back in range(12):
            moved = pltpu.roll(values, (first - back) % 16 * 8, 1)
            for x in range(2):
                y = back - 4 * x
                if 0 <= y < 8:
                    inside = lane == first + 4 * x
                    turned[y] = moved if k == 0 and x == 0 else jnp.where(inside, moved, turned[y])
    out_ref[...] = turned[...].astype(BF)
    fetch.wait()
    half = PLANES // 2
    slab = lax.axis_index("slab")
    here = home_ref[0:1, :] // half == slab
    place = (home_ref[0:1, :] - slab * half) * 2 + 16 * home_ref[1:2, :] + 256 * home_ref[2:3, :]
    place = jnp.where(here, place, 0)
    here = jnp.where(here, BLOCK_LIMIT / QMAX, 0.0)
    for r in range(place_ref.shape[0]):
        part = place[:, r * NG : (r + 1) * NG]
        total = part
        for t in range(1, atoms):
            total = total + pltpu.roll(part, NG - t, 1)
        place_ref[r : r + 1, :] = total
        here_ref[r : r + 1, :] = here[:, r * NG : (r + 1) * NG]


def message_kernel(proj_ref, out_ref, rows):
    rows[...] = jnp.zeros_like(rows)
    rows[pl.ds(0, proj_ref.shape[1]), :] = proj_ref[0].astype(F32)
    total = rows.shape[1]
    count = out_ref.shape[0]
    for b in range(count):
        moved = pltpu.roll(rows[...], (total - b * (total // count)) % total, 1)
        out_ref[b] = moved[:, :NG].astype(BF)


def charge_kernel(home_hbm, proj_ref, block_ref, out_ref, home_ref, sem):
    fetch = pltpu.make_async_copy(home_hbm, home_ref, sem)
    fetch.start()
    slab = lax.axis_index("slab")
    owner = lax.axis_index("band") * SLABS + slab
    groups = proj_ref.shape[0]
    atoms = block_ref.shape[1] // CHANNEL_ROWS
    lane = lax.broadcasted_iota(jnp.int32, (CHANNEL_ROWS, NG), 1)
    weights = [jnp.zeros((CHANNEL_ROWS, NG), F32)] * atoms
    for b in range(groups):
        mine = pltpu.roll(proj_ref[b].astype(F32), (NG - slab * atoms) & (NG - 1), 1)
        for t in range(atoms):
            weights[t] = jnp.where(lane // SLABS == b, mine[:, t : t + 1], weights[t])
    pieces = []
    fetch.wait()
    for t in range(atoms):
        goes = (lane & (SLABS - 1)) == home_ref[0, owner * atoms + t] // (PLANES // 2)
        behind = pltpu.roll(weights[t], NG - SLABS, 1)
        pairs = [jnp.where(goes, weights[t] * other, 0.0) for other in (weights[t], behind)]
        pieces.append(jnp.concatenate(pairs, axis=1))
    weight = jnp.concatenate(pieces, axis=0)
    bound = jnp.sum(jnp.abs(weight), axis=0, keepdims=True) * BLOCK_LIMIT
    weight = jnp.transpose(weight * (QMAX / jnp.maximum(bound, 1e-30)))
    both = jnp.concatenate(split(weight), axis=1)
    values = [dot(both, jnp.concatenate([block_ref[y], block_ref[y]], axis=0)) for y in range(8)]
    values = jnp.swapaxes(jnp.round(jnp.stack(values)), 0, 1)
    half = weight.shape[0] // 2
    out_ref[...] = to_int16(jnp.concatenate([values[:half], values[half:]], axis=1))


def mark_kernel(in_ref, out_ref):
    out_ref[...] = jnp.zeros_like(out_ref)


def density_kernel(p, place_ref, here_ref, charge_ref, own_ref, next_ref, proj_ref, next_proj_ref, right_ref, left_ref, out_ref, field, scales):
    rows, owners = here_ref.shape[0], charge_ref.shape[0]
    count = owners // rows
    atoms = NG // count
    own_lane = lax.broadcasted_iota(jnp.int32, (count, NG), 1) // atoms == lax.broadcasted_iota(jnp.int32, (count, NG), 0)
    sizes = jnp.sum(jnp.abs(proj_ref[0].astype(F32) * next_proj_ref[0].astype(F32)), axis=0, keepdims=True)
    for r in range(rows):
        bound = sizes[:, r * NG : (r + 1) * NG] * here_ref[r : r + 1, :]
        total = jnp.sum(jnp.where(own_lane, bound, 0.0), axis=1, keepdims=True)
        scales[pl.ds(r * count, count), :] = jnp.broadcast_to(total, (count, NG))
    for x in range(PLANES):
        field[x] = own_ref[0, x].astype(F32) * next_ref[0, x].astype(F32)
    lane = lax.broadcasted_iota(jnp.int32, (8, NG), 1)

    def add_row(r, carry):
        for i in range(count):
            add_atom(r * count + i, place_ref[r, i * atoms])
        return carry

    def add_atom(d, place):
        plane = place & 15
        brick_y = (place >> 4) & 15
        shift = (place >> 8) * 8
        inside = ((lane - shift) & (NG - 1)) < 16
        places = []
        tile = from_int16(charge_ref[d])[8 * p : 8 * p + 8] * scales[pl.ds(d, 1), :]
        for g in range(8):
            turned = pltpu.roll(tile, (shift + (NG - 16 * g)) & (NG - 1), 1)
            row = pl.multiple_of(((brick_y + g % 2) & (NG // 8 - 1)) * 8, 8)
            at = (plane + g // 2, pl.ds(row, 8))
            places.append((at, field[at] + jnp.where(inside, turned, 0.0)))
        for at, total in places:
            field[at] = total

    lax.fori_loop(0, rows, add_row, 0)
    for x in range(0, PLANES, 2):
        both = times_right(jnp.concatenate([field[x], field[x + 1]], axis=0), right_ref)
        both = times_left(left_ref, jnp.concatenate([both[:NG], both[NG:]], axis=1))
        field[x] = both[:, :NG]
        field[x + 1] = both[:, NG:]

    def pack(d, carry):
        rows = pl.ds(pl.multiple_of(d * ROWS, ROWS), ROWS)
        largest = jnp.abs(field[0, rows])
        for x in range(1, PLANES):
            largest = jnp.maximum(largest, jnp.abs(field[x, rows]))
        code = step_code(largest)
        factor = 1.0 / step_size(code)
        lows = []
        for x in range(PLANES):
            scaled = field[x, rows] * factor
            whole = jnp.round(scaled)
            out_ref[d, x] = to_int16(whole)
            lows.append((scaled - whole)[0:1])
        out_ref[d, PLANES] = to_int16(code)
        low = jnp.concatenate(lows, axis=0) * (2.0 * QMAX)
        out_ref[d, PLANES + 1] = to_int16(jnp.round(low))
        return carry

    lax.fori_loop(0, SLABS, pack, 0, unroll=True)


def solve_kernel(base, squares_ref, in_ref, fold_x_ref, fold_z_ref, left_ref, *rest):
    *more, out_ref, field = rest

    for s in range(SLABS):
        step = step_size(from_int16(in_ref[s, base + PLANES]))
        planes = from_int16(in_ref[s, pl.ds(base, PLANES)]) * step[None]
        low = from_int16(in_ref[s, base + PLANES + 1]) * (step[0:1] * (0.5 / QMAX))
        rows = pl.ds(s * PLANES, PLANES)
        field[:, rows, :] = jnp.swapaxes(planes, 0, 1)
        field[0, rows, :] = field[0, rows, :] + low
    fold = fold_x_ref[...] + fold_z_ref[...]
    slab = lax.axis_index("slab")
    for r in range(0, ROWS, 2):
        halves = []
        for k in range(2):
            total = fold + squares_ref[slab, r + k]
            halves.append(jnp.where(total > 0, KERNEL_SCALE / (total + SCREENING_RANGE), 0.0) * (1.0 / NG**3))
        columns = jnp.concatenate([field[r], field[r + 1]], axis=1)
        spectrum = times_left(left_ref, columns) * jnp.concatenate(halves, axis=1)
        columns = times_left(left_ref, spectrum)
        field[r] = columns[:, :NG]
        field[r + 1] = columns[:, NG:]
    for s in range(SLABS):
        planes = jnp.swapaxes(field[:, pl.ds(s * PLANES, PLANES), :], 0, 1)
        code = step_code(jnp.max(jnp.abs(planes), axis=0))
        out_ref[s, pl.ds(0, PLANES)] = to_int16(jnp.round(planes * (1.0 / step_size(code))[None]))
        out_ref[s, PLANES] = to_int16(code)
        for more_ref in more:
            out_ref[s, pl.ds(BACK_TILES, FWD_TILES)] = more_ref[s]


def potential_pair(in_ref, steps, x, left_ref, right_ref):
    halves = []
    for k in range(2):
        halves.append(jnp.concatenate([from_int16(in_ref[s, x + k]) * steps[s] for s in range(SLABS)], axis=0))
    both = times_left(left_ref, jnp.concatenate(halves, axis=1))
    both = times_right(jnp.concatenate([both[:, :NG], both[:, NG:]], axis=0), right_ref)
    return both[:NG], both[NG:]


def back_cross_kernel(in_ref, own_ref, next_ref, left_ref, right_ref, kept_ref, sent_ref, codes):
    steps = [step_size(from_int16(in_ref[s, PLANES])) for s in range(SLABS)]
    for x in range(0, PLANES, 2):
        pair = potential_pair(in_ref, steps, x, left_ref, right_ref)
        for k in range(2):
            potential = pair[k]
            kept_ref[x + k] = potential * next_ref[0, x + k].astype(F32)
            product = potential * own_ref[0, x + k].astype(F32)
            code = step_code(jnp.max(jnp.abs(product), axis=0, keepdims=True))
            codes[x + k : x + k + 1, :] = code
            sent_ref[pl.ds((x + k) * NG, NG), :] = to_int16(jnp.round(product * (1.0 / step_size(code))))
    sent_ref[pl.ds(PLANES * NG, PLANES), :] = to_int16(codes[...])


def back_own_kernel(in_ref, own_ref, kept_ref, sent_ref, left_ref, right_ref, out_ref):
    steps = [step_size(from_int16(in_ref[s, PLANES])) for s in range(SLABS)]
    sent_steps = step_size(from_int16(sent_ref[pl.ds(PLANES * NG, PLANES), :]))
    for x in range(0, PLANES, 2):
        pair = potential_pair(in_ref, steps, x, left_ref, right_ref)
        for k in range(2):
            sent = from_int16(sent_ref[pl.ds((x + k) * NG, NG), :]) * sent_steps[x + k : x + k + 1]
            out_ref[0, x + k] = kept_ref[x + k] + sent + pair[k] * own_ref[0, x + k].astype(F32)


def hbm():
    return pl.BlockSpec(memory_space=pltpu.HBM)


def vmem():
    return pl.BlockSpec(memory_space=pltpu.VMEM)


def smem():
    return pl.BlockSpec(memory_space=pltpu.SMEM)


def call(kernel, in_specs, out_shape, scratch, name, micros):
    many = isinstance(out_shape, (list, tuple))
    return pl.pallas_call(
        kernel,
        in_specs=in_specs,
        out_specs=[vmem() for _ in out_shape] if many else vmem(),
        out_shape=out_shape,
        scratch_shapes=scratch,
        name=name,
        cost_estimate=pl.CostEstimate(
            flops=int(micros * 1e8), bytes_accessed=int(micros * 3.5e6), transcendentals=0
        ),
        compiler_params=pltpu.CompilerParams(vmem_limit_bytes=VMEM_LIMIT),
    )


def mark(array):
    whole = [pl.BlockSpec(memory_space=pl.ANY)]
    return call(mark_kernel, whole, jax.ShapeDtypeStruct((8, NG), F32), [], "mark", 30)(array)


def from_behind(block, axis, distance):
    count = lax.axis_size(axis)
    return lax.ppermute(block, axis, [((i - distance) % count, i) for i in range(count)])


def per_device(orbitals, projections, aug_blocks, atom_home):
    n_band = lax.axis_size("band")
    n_slab = lax.axis_size("slab")
    owners = n_band * n_slab
    atom_dev = aug_blocks.shape[0]
    right, left, left_y, left_y_back = (jnp.asarray(t) for t in tables())
    squares = fold_square_host()


    messages = call(
        message_kernel,
        [vmem()],
        jax.ShapeDtypeStruct((n_band, CHANNEL_ROWS, NG), BF),
        [pltpu.VMEM((CHANNEL_ROWS, projections.shape[2]), F32)],
        "messages",
        1,
    )(projections)
    all_proj = lax.all_to_all(messages, "band", split_axis=0, concat_axis=0, tiled=True)

    home_rows = atom_home.shape[1] // NG
    blocks, places, here = call(
        local_kernel,
        [pl.BlockSpec(memory_space=pl.ANY), hbm(), vmem()],
        [
            jax.ShapeDtypeStruct((8, atom_dev * CHANNEL_ROWS, NG), BF),
            jax.ShapeDtypeStruct((home_rows, NG), jnp.int32),
            jax.ShapeDtypeStruct((home_rows, NG), F32),
        ],
        [pltpu.VMEM((8, atom_dev * CHANNEL_ROWS, NG), F32)] * 2
        + [pltpu.VMEM(atom_home.shape, jnp.int32), pltpu.SemaphoreType.DMA],
        "local",
        1,
    )(messages, atom_home, aug_blocks.transpose(0, 2, 1, 3))
    own, proj, blocks = lax.optimization_barrier((orbitals, projections, blocks))
    next_proj = from_behind(proj, "band", -1)
    nxt = from_behind(own, "band", -1)

    charges = call(
        charge_kernel,
        [hbm()] + [vmem()] * 2,
        jax.ShapeDtypeStruct((owners, 16, NG), jnp.int16),
        [pltpu.SMEM(atom_home.shape, jnp.int32), pltpu.SemaphoreType.DMA],
        "charges",
        2,
    )(atom_home, all_proj, blocks)
    charges = lax.all_to_all(charges, ("band", "slab"), split_axis=0, concat_axis=0, tiled=True)

    fold_y = jnp.asarray(squares[row_order()])
    fold_x = jnp.asarray(np.broadcast_to(squares[:, None], (NG, NG)).copy())
    fold_z = jnp.asarray(squares[None, :])

    def density(p, other, other_proj):
        return call(
            functools.partial(density_kernel, p),
            [smem()] + [vmem()] * 8,
            jax.ShapeDtypeStruct((n_slab, FWD_TILES, 16, NG), jnp.int16),
            [pltpu.VMEM((PLANES, NG, NG), F32), pltpu.VMEM((owners, NG), F32)],
            "density" + str(p),
            6,
        )(places, here, charges, own, other, proj, other_proj, right, left_y)

    def solve(name, base, spectrum, *more):
        tiles = BACK_TILES + FWD_TILES * len(more)
        return call(
            functools.partial(solve_kernel, base),
            [smem()] + [vmem()] * (4 + len(more)),
            jax.ShapeDtypeStruct((n_slab, tiles, 16, NG), jnp.int16),
            [pltpu.VMEM((ROWS, NG, NG), F32)],
            name,
            3,
        )(fold_y, spectrum, fold_x, fold_z, left, *more)

    def swap(block):
        return lax.all_to_all(block, "slab", split_axis=0, concat_axis=0, tiled=True)

    cross = swap(density(1, nxt, next_proj))
    cross = swap(solve("solve1", 0, cross, density(0, own, proj)))
    mine = swap(solve("solve0", BACK_TILES, cross))

    kept, sent = call(
        back_cross_kernel,
        [vmem()] * 5,
        [
            jax.ShapeDtypeStruct((PLANES, NG, NG), F32),
            jax.ShapeDtypeStruct((PLANES * NG + PLANES, NG), jnp.int16),
        ],
        [pltpu.VMEM((PLANES, NG), F32)],
        "back_cross",
        2,
    )(cross, own, nxt, left_y_back, right)
    got = from_behind(sent, "band", 1)
    got, _ = lax.optimization_barrier((got, mark(mine)))
    return call(
        back_own_kernel,
        [vmem()] * 6,
        jax.ShapeDtypeStruct((1, PLANES, NG, NG), F32),
        [],
        "back_own",
        2,
    )(mine, own, kept, got, left_y_back, right)


def solution(mesh):
    in_specs = (
        P("band", "slab", None, None),
        P("band", None, None),
        P(("band", "slab"), None, None, None),
        P(),
    )
    out_specs = P("band", "slab", None, None)
    return jax.shard_map(
        per_device, mesh=mesh, in_specs=in_specs, out_specs=out_specs, check_vma=False
    )
```

```python
import functools
import math

import numpy as np
import jax
import jax.numpy as jnp
from jax import lax
from jax.experimental import pallas as pl
from jax.experimental.pallas import tpu as pltpu
from jax.sharding import PartitionSpec as P

KERNEL_SCALE = 0.5
SCREENING_RANGE = 0.002
NG = 128
SLABS = 8
ROWS = NG // SLABS
PLANES = NG // SLABS
BLOCK_LIMIT = 3.0
QMAX = 32760.0
STEPS = 8.0
CHANNEL_ROWS = 16
FWD_TILES = PLANES + 2
BACK_TILES = PLANES + 1
BF = jnp.bfloat16
F32 = jnp.float32
VMEM_LIMIT = 50 * 1024 * 1024


def hartley_host():
    index = np.arange(NG)
    angle = (index[:, None] * index[None, :] % NG) * (2.0 * math.pi / NG)
    return (np.cos(angle) + np.sin(angle)).astype(np.float32)


def split_host(table):
    high = table.astype(jnp.bfloat16)
    low = (table - high.astype(np.float32)).astype(jnp.bfloat16)
    return high, low


def row_order():
    by_size = sorted(range(NG), key=lambda k: (min(k, NG - k), k))
    return np.array([[by_size[d + SLABS * r] for r in range(ROWS)] for d in range(SLABS)])


def fold_square_host():
    index = np.arange(NG)
    return ((np.minimum(index, NG - index)).astype(np.float32) * np.float32(2.0 * math.pi / NG)) ** 2


def tables():
    table = hartley_host()
    high, low = split_host(table)
    order = row_order().reshape(-1)
    high_y, low_y = high[order], low[order]
    top = np.concatenate([high, low], axis=1)
    bottom = np.concatenate([high, np.zeros_like(high)], axis=1)
    right = np.concatenate([top, bottom], axis=0)
    left = np.concatenate([high, low, high], axis=1)
    left_y = np.concatenate([high_y, low_y, high_y], axis=1)
    left_y_back = np.concatenate([high_y.T, low_y.T, high_y.T], axis=1)
    return right, left, left_y, left_y_back


def split(value):
    high = value.astype(BF)
    low = (value - high.astype(F32)).astype(BF)
    return high, low


def dot(a, b):
    return jnp.dot(a, b, preferred_element_type=F32)


def times_right(value, right_ref):
    high, low = split(value)
    both = dot(jnp.concatenate([high, low], axis=1), right_ref[...])
    return both[:, :NG] + both[:, NG:]


def times_left(left_ref, value):
    high, low = split(value)
    return dot(left_ref[...], jnp.concatenate([high, high, low], axis=0))


def step_code(largest):
    return jnp.ceil(jnp.log(jnp.maximum(largest, 1e-30)) * (STEPS / math.log(2.0)))


def step_size(code):
    return jnp.exp(code * (math.log(2.0) / STEPS)) * (1.001 / QMAX)


def to_int16(value):
    return value.astype(jnp.int32).astype(jnp.int16)


def from_int16(value):
    return value.astype(jnp.int32).astype(F32)


def local_kernel(after_ref, home_any, block_ref, out_ref, place_ref, here_ref, goes_ref, rows, turned, home_ref, sem):
    fetch = pltpu.make_async_copy(home_any, home_ref, sem)
    fetch.start()
    lane = lax.broadcasted_iota(jnp.int32, (1, NG), 1) // 8
    atoms, channels, bricks = block_ref.shape[:3]
    rows[...] = jnp.zeros_like(rows)
    for t in range(atoms):
        rows[:, pl.ds(CHANNEL_ROWS * t, channels), :] = jnp.swapaxes(block_ref[t].astype(F32), 0, 1)
    for k in range(bricks):
        values = rows[k]
        first = (k // 4) * 8 + (k // 2 % 2) * 2 + k % 2
        for back in range(12):
            moved = pltpu.roll(values, (first - back) % 16 * 8, 1)
            for x in range(2):
                y = back - 4 * x
                if 0 <= y < 8:
                    inside = lane == first + 4 * x
                    turned[y] = moved if k == 0 and x == 0 else jnp.where(inside, moved, turned[y])
    out_ref[...] = turned[...].astype(BF)
    fetch.wait()
    half = PLANES // 2
    slab = lax.axis_index("slab")
    here = home_ref[0:1, :] // half == slab
    place = (home_ref[0:1, :] - slab * half) * 2 + 16 * home_ref[1:2, :] + 256 * home_ref[2:3, :]
    place = jnp.where(here, place, 0)
    here = jnp.where(here, BLOCK_LIMIT / QMAX, 0.0)
    for r in range(place_ref.shape[0]):
        part = place[:, r * NG : (r + 1) * NG]
        total = part
        for t in range(1, atoms):
            total = total + pltpu.roll(part, NG - t, 1)
        place_ref[r : r + 1, :] = total
        here_ref[r : r + 1, :] = here[:, r * NG : (r + 1) * NG]
    owner = lax.axis_index("band") * SLABS + slab
    wide = home_ref.shape[1]
    mine = pltpu.roll(home_ref[0:1, :] // half, wide - owner * atoms, 1)[:, :NG]
    slab_lane = lax.broadcasted_iota(jnp.int32, (1, NG), 1) & (SLABS - 1)
    for t in range(atoms):
        goes_ref[t : t + 1, :] = jnp.where(mine[:, t : t + 1] == slab_lane, 1.0, 0.0)


def message_kernel(proj_ref, out_ref, rows):
    rows[...] = jnp.zeros_like(rows)
    rows[pl.ds(0, proj_ref.shape[1]), :] = proj_ref[0].astype(F32)
    total = rows.shape[1]
    count = out_ref.shape[0]
    for b in range(count):
        moved = pltpu.roll(rows[...], (total - b * (total // count)) % total, 1)
        out_ref[b] = moved[:, :NG].astype(BF)


def streamed(out_ref, held, sems, chunk, start, size):
    part = pl.ds(start, size)
    copy = pltpu.make_async_copy(held.at[part], out_ref.at[part], sems.at[chunk])
    copy.start()
    return copy


def charge_kernel(goes_ref, proj_ref, block_ref, out_ref, held, sems):
    slab = lax.axis_index("slab")
    groups = proj_ref.shape[0]
    atoms = block_ref.shape[1] // CHANNEL_ROWS
    lane = lax.broadcasted_iota(jnp.int32, (CHANNEL_ROWS, NG), 1)
    weights = [jnp.zeros((CHANNEL_ROWS, NG), F32)] * atoms
    for b in range(groups):
        mine = pltpu.roll(proj_ref[b].astype(F32), (NG - slab * atoms) & (NG - 1), 1)
        for t in range(atoms):
            weights[t] = jnp.where(lane // SLABS == b, mine[:, t : t + 1], weights[t])
    pieces = []
    for t in range(atoms):
        behind = pltpu.roll(weights[t], NG - SLABS, 1)
        picked = weights[t] * goes_ref[t : t + 1, :]
        pieces.append(jnp.concatenate([picked * weights[t], picked * behind], axis=1))
    weight = jnp.concatenate(pieces, axis=0)
    bound = jnp.sum(jnp.abs(weight), axis=0, keepdims=True) * BLOCK_LIMIT
    weight = jnp.transpose(weight * (QMAX / jnp.maximum(bound, 1e-30)))
    both = jnp.concatenate(split(weight), axis=1)
    half = weight.shape[0] // 2
    size = half // 4
    copies = []
    blocks = [jnp.concatenate([block_ref[y], block_ref[y]], axis=0) for y in range(8)]
    for n in range(4):
        pairs = []
        for p in range(2):
            rows = both[p * half + n * size : p * half + (n + 1) * size]
            values = jnp.round(jnp.stack([dot(rows, block) for block in blocks]))
            pairs.append(jnp.swapaxes(values, 0, 1))
        held[pl.ds(n * size, size)] = to_int16(jnp.concatenate(pairs, axis=1))
        copies.append(streamed(out_ref, held, sems, n, n * size, size))
    for copy in copies:
        copy.wait()


def density_kernel(p, place_vmem, here_ref, charge_ref, own_ref, next_ref, proj_ref, next_proj_ref, right_ref, left_ref, out_ref, field, scales, place_ref, sem):
    fetch = pltpu.make_async_copy(place_vmem, place_ref, sem)
    fetch.start()
    rows, owners = here_ref.shape[0], charge_ref.shape[0]
    count = owners // rows
    atoms = NG // count
    own_lane = lax.broadcasted_iota(jnp.int32, (count, NG), 1) // atoms == lax.broadcasted_iota(jnp.int32, (count, NG), 0)
    sizes = jnp.sum(jnp.abs(proj_ref[0].astype(F32) * next_proj_ref[0].astype(F32)), axis=0, keepdims=True)
    for r in range(rows):
        bound = sizes[:, r * NG : (r + 1) * NG] * here_ref[r : r + 1, :]
        total = jnp.sum(jnp.where(own_lane, bound, 0.0), axis=1, keepdims=True)
        scales[pl.ds(r * count, count), :] = jnp.broadcast_to(total, (count, NG))
    for x in range(PLANES):
        field[x] = own_ref[0, x].astype(F32) * next_ref[0, x].astype(F32)
    lane = lax.broadcasted_iota(jnp.int32, (8, NG), 1)
    fetch.wait()

    def add_row(r, carry):
        for i in range(count):
            add_atom(r * count + i, place_ref[r, i * atoms])
        return carry

    def add_atom(d, place):
        plane = place & 15
        brick_y = (place >> 4) & 15
        shift = (place >> 8) * 8
        inside = ((lane - shift) & (NG - 1)) < 16
        places = []
        tile = from_int16(charge_ref[d])[8 * p : 8 * p + 8] * scales[pl.ds(d, 1), :]
        for g in range(8):
            turned = pltpu.roll(tile, (shift + (NG - 16 * g)) & (NG - 1), 1)
            row = pl.multiple_of(((brick_y + g % 2) & (NG // 8 - 1)) * 8, 8)
            at = (plane + g // 2, pl.ds(row, 8))
            places.append((at, field[at] + jnp.where(inside, turned, 0.0)))
        for at, total in places:
            field[at] = total

    lax.fori_loop(0, rows, add_row, 0)
    for x in range(0, PLANES, 2):
        both = times_right(jnp.concatenate([field[x], field[x + 1]], axis=0), right_ref)
        both = times_left(left_ref, jnp.concatenate([both[:NG], both[NG:]], axis=1))
        field[x] = both[:, :NG]
        field[x + 1] = both[:, NG:]

    for d in range(SLABS):
        rows = pl.ds(d * ROWS, ROWS)
        largest = jnp.abs(field[0, rows])
        for x in range(1, PLANES):
            largest = jnp.maximum(largest, jnp.abs(field[x, rows]))
        code = step_code(largest)
        factor = 1.0 / step_size(code)
        lows = []
        for x in range(PLANES):
            scaled = field[x, rows] * factor
            whole = jnp.round(scaled)
            out_ref[d, x] = to_int16(whole)
            lows.append((scaled - whole)[0:1])
        out_ref[d, PLANES] = to_int16(code)
        low = jnp.concatenate(lows, axis=0) * (2.0 * QMAX)
        out_ref[d, PLANES + 1] = to_int16(jnp.round(low))


def solve_kernel(base, squares_ref, in_ref, fold_x_ref, fold_z_ref, left_ref, *rest):
    *more, out_ref, field = rest

    for s in range(SLABS):
        step = step_size(from_int16(in_ref[s, base + PLANES]))
        planes = from_int16(in_ref[s, pl.ds(base, PLANES)]) * step[None]
        low = from_int16(in_ref[s, base + PLANES + 1]) * (step[0:1] * (0.5 / QMAX))
        rows = pl.ds(s * PLANES, PLANES)
        field[:, rows, :] = jnp.swapaxes(planes, 0, 1)
        field[0, rows, :] = field[0, rows, :] + low
    fold = fold_x_ref[...] + fold_z_ref[...]
    squares = squares_ref[pl.ds(lax.axis_index("slab"), 1), :]
    for r in range(0, ROWS, 2):
        halves = []
        for k in range(2):
            total = fold + squares[:, r + k : r + k + 1]
            halves.append(jnp.where(total > 0, KERNEL_SCALE / (total + SCREENING_RANGE), 0.0) * (1.0 / NG**3))
        columns = jnp.concatenate([field[r], field[r + 1]], axis=1)
        spectrum = times_left(left_ref, columns) * jnp.concatenate(halves, axis=1)
        columns = times_left(left_ref, spectrum)
        field[r] = columns[:, :NG]
        field[r + 1] = columns[:, NG:]
    for s in range(SLABS):
        planes = jnp.swapaxes(field[:, pl.ds(s * PLANES, PLANES), :], 0, 1)
        code = step_code(jnp.max(jnp.abs(planes), axis=0))
        out_ref[s, pl.ds(0, PLANES)] = to_int16(jnp.round(planes * (1.0 / step_size(code))[None]))
        out_ref[s, PLANES] = to_int16(code)
        for more_ref in more:
            out_ref[s, pl.ds(BACK_TILES, FWD_TILES)] = more_ref[s]


def potential_pair(in_ref, steps, x, left_ref, right_ref):
    halves = []
    for k in range(2):
        halves.append(jnp.concatenate([from_int16(in_ref[s, x + k]) * steps[s] for s in range(SLABS)], axis=0))
    both = times_left(left_ref, jnp.concatenate(halves, axis=1))
    both = times_right(jnp.concatenate([both[:, :NG], both[:, NG:]], axis=0), right_ref)
    return both[:NG], both[NG:]


def back_cross_kernel(in_ref, own_ref, next_ref, left_ref, right_ref, kept_ref, sent_ref, codes):
    steps = [step_size(from_int16(in_ref[s, PLANES])) for s in range(SLABS)]
    for x in range(0, PLANES, 2):
        pair = potential_pair(in_ref, steps, x, left_ref, right_ref)
        for k in range(2):
            potential = pair[k]
            kept_ref[x + k] = potential * next_ref[0, x + k].astype(F32)
            product = potential * own_ref[0, x + k].astype(F32)
            code = step_code(jnp.max(jnp.abs(product), axis=0, keepdims=True))
            codes[x + k : x + k + 1, :] = code
            sent_ref[pl.ds((x + k) * NG, NG), :] = to_int16(jnp.round(product * (1.0 / step_size(code))))
    sent_ref[pl.ds(PLANES * NG, PLANES), :] = to_int16(codes[...])


def back_own_kernel(in_ref, own_ref, kept_ref, sent_ref, left_ref, right_ref, out_ref, held, sems):
    copies = []
    steps = [step_size(from_int16(in_ref[s, PLANES])) for s in range(SLABS)]
    sent_steps = step_size(from_int16(sent_ref[pl.ds(PLANES * NG, PLANES), :]))
    for x in range(0, PLANES, 2):
        pair = potential_pair(in_ref, steps, x, left_ref, right_ref)
        for k in range(2):
            sent = from_int16(sent_ref[pl.ds((x + k) * NG, NG), :]) * sent_steps[x + k : x + k + 1]
            held[x + k] = kept_ref[x + k] + sent + pair[k] * own_ref[0, x + k].astype(F32)
        copies.append(streamed(out_ref.at[0], held, sems, x // 2, x, 2))
    for copy in copies:
        copy.wait()


def hbm():
    return pl.BlockSpec(memory_space=pltpu.HBM)


def vmem():
    return pl.BlockSpec(memory_space=pltpu.VMEM)


def smem():
    return pl.BlockSpec(memory_space=pltpu.SMEM)


def call(kernel, in_specs, out_shape, scratch, name, micros, out_specs=None):
    many = isinstance(out_shape, (list, tuple))
    out_specs = out_specs or [vmem()] * (len(out_shape) if many else 1)
    return pl.pallas_call(
        kernel,
        in_specs=in_specs,
        out_specs=out_specs if many else out_specs[0],
        out_shape=out_shape,
        scratch_shapes=scratch,
        name=name,
        cost_estimate=pl.CostEstimate(
            flops=int(micros * 1e8), bytes_accessed=int(micros * 3.5e6), transcendentals=0
        ),
        compiler_params=pltpu.CompilerParams(vmem_limit_bytes=VMEM_LIMIT),
    )


def from_behind(block, axis, distance):
    count = lax.axis_size(axis)
    return lax.ppermute(block, axis, [((i - distance) % count, i) for i in range(count)])


def per_device(orbitals, projections, aug_blocks, atom_home):
    n_band = lax.axis_size("band")
    n_slab = lax.axis_size("slab")
    owners = n_band * n_slab
    atom_dev = aug_blocks.shape[0]
    right, left, left_y, left_y_back = (jnp.asarray(t) for t in tables())
    squares = fold_square_host()


    messages = call(
        message_kernel,
        [vmem()],
        jax.ShapeDtypeStruct((n_band, CHANNEL_ROWS, NG), BF),
        [pltpu.VMEM((CHANNEL_ROWS, projections.shape[2]), F32)],
        "messages",
        1,
    )(projections)
    all_proj = lax.all_to_all(messages, "band", split_axis=0, concat_axis=0, tiled=True)

    home_rows = atom_home.shape[1] // NG
    blocks, places, here, goes = call(
        local_kernel,
        [pl.BlockSpec(memory_space=pl.ANY), hbm(), vmem()],
        [
            jax.ShapeDtypeStruct((8, atom_dev * CHANNEL_ROWS, NG), BF),
            jax.ShapeDtypeStruct((home_rows, NG), jnp.int32),
            jax.ShapeDtypeStruct((home_rows, NG), F32),
            jax.ShapeDtypeStruct((atom_dev, NG), F32),
        ],
        [pltpu.VMEM((8, atom_dev * CHANNEL_ROWS, NG), F32)] * 2
        + [pltpu.VMEM(atom_home.shape, jnp.int32), pltpu.SemaphoreType.DMA],
        "local",
        1,
    )(messages, atom_home, aug_blocks.transpose(0, 2, 1, 3))
    own, proj, blocks = lax.optimization_barrier((orbitals, projections, blocks))
    next_proj = from_behind(proj, "band", -1)
    nxt = from_behind(own, "band", -1)

    charges = call(
        charge_kernel,
        [vmem()] * 3,
        jax.ShapeDtypeStruct((owners, 16, NG), jnp.int16),
        [pltpu.VMEM((owners, 16, NG), jnp.int16), pltpu.SemaphoreType.DMA((4,))],
        "charges",
        2,
        [hbm()],
    )(goes, all_proj, blocks)
    charges = lax.all_to_all(charges, ("band", "slab"), split_axis=0, concat_axis=0, tiled=True)

    fold_y = jnp.asarray(squares[row_order()])
    fold_x = jnp.asarray(np.broadcast_to(squares[:, None], (NG, NG)).copy())
    fold_z = jnp.asarray(squares[None, :])

    def density(p, other, other_proj):
        return call(
            functools.partial(density_kernel, p),
            [vmem()] * 9,
            jax.ShapeDtypeStruct((n_slab, FWD_TILES, 16, NG), jnp.int16),
            [
                pltpu.VMEM((PLANES, NG, NG), F32),
                pltpu.VMEM((owners, NG), F32),
                pltpu.SMEM(places.shape, jnp.int32),
                pltpu.SemaphoreType.DMA,
            ],
            "density" + str(p),
            6,
        )(places, here, charges, own, other, proj, other_proj, right, left_y)

    def solve(name, base, spectrum, *more):
        tiles = BACK_TILES + FWD_TILES * len(more)
        return call(
            functools.partial(solve_kernel, base),
            [vmem()] * (5 + len(more)),
            jax.ShapeDtypeStruct((n_slab, tiles, 16, NG), jnp.int16),
            [pltpu.VMEM((ROWS, NG, NG), F32)],
            name,
            3,
        )(fold_y, spectrum, fold_x, fold_z, left, *more)

    def swap(block):
        return lax.all_to_all(block, "slab", split_axis=0, concat_axis=0, tiled=True)

    cross = swap(density(1, nxt, next_proj))
    cross = swap(solve("solve1", 0, cross, density(0, own, proj)))
    mine = swap(solve("solve0", BACK_TILES, cross))

    kept, sent = call(
        back_cross_kernel,
        [vmem()] * 5,
        [
            jax.ShapeDtypeStruct((PLANES, NG, NG), F32),
            jax.ShapeDtypeStruct((PLANES * NG + PLANES, NG), jnp.int16),
        ],
        [pltpu.VMEM((PLANES, NG), F32)],
        "back_cross",
        2,
    )(cross, own, nxt, left_y_back, right)
    got = from_behind(sent, "band", 1)
    return call(
        back_own_kernel,
        [vmem()] * 6,
        jax.ShapeDtypeStruct((1, PLANES, NG, NG), F32),
        [pltpu.VMEM((PLANES, NG, NG), F32), pltpu.SemaphoreType.DMA((PLANES // 2,))],
        "back_own",
        2,
        [hbm()],
    )(mine, own, kept, got, left_y_back, right)


def solution(mesh):
    in_specs = (
        P("band", "slab", None, None),
        P("band", None, None),
        P(("band", "slab"), None, None, None),
        P(),
    )
    out_specs = P("band", "slab", None, None)
    return jax.shard_map(
        per_device, mesh=mesh, in_specs=in_specs, out_specs=out_specs, check_vma=False
    )
```

```python
import functools
import math

import numpy as np
import jax
import jax.numpy as jnp
from jax import lax
from jax.experimental import pallas as pl
from jax.experimental.pallas import tpu as pltpu
from jax.sharding import PartitionSpec as P

KERNEL_SCALE = 0.5
SCREENING_RANGE = 0.002
NG = 128
SLABS = 8
ROWS = NG // SLABS
PLANES = NG // SLABS
BLOCK_LIMIT = 3.0
QMAX = 32760.0
STEPS = 8.0
CHANNEL_ROWS = 16
ROUND = (0, 2, 4, 6, 7, 5, 3, 1)
FWD_TILES = PLANES + 2
BACK_TILES = PLANES + 1
BF = jnp.bfloat16
F32 = jnp.float32
VMEM_LIMIT = 50 * 1024 * 1024


def hartley_host():
    index = np.arange(NG)
    angle = (index[:, None] * index[None, :] % NG) * (2.0 * math.pi / NG)
    return (np.cos(angle) + np.sin(angle)).astype(np.float32)


def split_host(table):
    high = table.astype(jnp.bfloat16)
    low = (table - high.astype(np.float32)).astype(jnp.bfloat16)
    return high, low


def row_order():
    by_size = sorted(range(NG), key=lambda k: (min(k, NG - k), k))
    return np.array([[by_size[d + SLABS * r] for r in range(ROWS)] for d in range(SLABS)])


def fold_square_host():
    index = np.arange(NG)
    return ((np.minimum(index, NG - index)).astype(np.float32) * np.float32(2.0 * math.pi / NG)) ** 2


def tables():
    table = hartley_host()
    high, low = split_host(table)
    order = row_order()[list(ROUND)].reshape(-1)
    high_y, low_y = high[order], low[order]
    top = np.concatenate([high, low], axis=1)
    bottom = np.concatenate([high, np.zeros_like(high)], axis=1)
    right = np.concatenate([top, bottom], axis=0)
    left = np.concatenate([high, low, high], axis=1)
    left_y = np.concatenate([high_y, low_y, high_y], axis=1)
    left_y_back = np.concatenate([high_y.T, low_y.T, high_y.T], axis=1)
    return right, left, left_y, left_y_back


def split(value):
    high = value.astype(BF)
    low = (value - high.astype(F32)).astype(BF)
    return high, low


def dot(a, b):
    return jnp.dot(a, b, preferred_element_type=F32)


def times_right(value, right_ref):
    high, low = split(value)
    both = dot(jnp.concatenate([high, low], axis=1), right_ref[...])
    return both[:, :NG] + both[:, NG:]


def times_left(left_ref, value):
    high, low = split(value)
    return dot(left_ref[...], jnp.concatenate([high, high, low], axis=0))


def step_code(largest):
    return jnp.ceil(jnp.log(jnp.maximum(largest, 1e-30)) * (STEPS / math.log(2.0)))


def step_size(code):
    return jnp.exp(code * (math.log(2.0) / STEPS)) * (1.001 / QMAX)


def to_int16(value):
    return value.astype(jnp.int32).astype(jnp.int16)


def from_int16(value):
    return value.astype(jnp.int32).astype(F32)


def local_kernel(after_ref, home_any, block_ref, out_ref, place_ref, here_ref, goes_ref, rows, turned, home_ref, sem):
    fetch = pltpu.make_async_copy(home_any, home_ref, sem)
    fetch.start()
    lane = lax.broadcasted_iota(jnp.int32, (1, NG), 1) // 8
    atoms, channels, bricks = block_ref.shape[:3]
    rows[...] = jnp.zeros_like(rows)
    for t in range(atoms):
        rows[:, pl.ds(CHANNEL_ROWS * t, channels), :] = jnp.swapaxes(block_ref[t].astype(F32), 0, 1)
    for k in range(bricks):
        values = rows[k]
        first = (k // 4) * 8 + (k // 2 % 2) * 2 + k % 2
        for back in range(12):
            moved = pltpu.roll(values, (first - back) % 16 * 8, 1)
            for x in range(2):
                y = back - 4 * x
                if 0 <= y < 8:
                    inside = lane == first + 4 * x
                    turned[y] = moved if k == 0 and x == 0 else jnp.where(inside, moved, turned[y])
    out_ref[...] = turned[...].astype(BF)
    fetch.wait()
    half = PLANES // 2
    slab = lax.axis_index("slab")
    here = home_ref[0:1, :] // half == slab
    place = (home_ref[0:1, :] - slab * half) * 2 + 16 * home_ref[1:2, :] + 256 * home_ref[2:3, :]
    place = jnp.where(here, place, 0)
    here = jnp.where(here, BLOCK_LIMIT / QMAX, 0.0)
    for r in range(place_ref.shape[0]):
        part = place[:, r * NG : (r + 1) * NG]
        total = part
        for t in range(1, atoms):
            total = total + pltpu.roll(part, NG - t, 1)
        place_ref[r : r + 1, :] = total
        here_ref[r : r + 1, :] = here[:, r * NG : (r + 1) * NG]
    owner = lax.axis_index("band") * SLABS + slab
    wide = home_ref.shape[1]
    mine = pltpu.roll(home_ref[0:1, :] // half, (wide - owner * atoms) & (wide - 1), 1)[:, :NG]
    slab_lane = lax.broadcasted_iota(jnp.int32, (1, NG), 1) & (SLABS - 1)
    for t in range(atoms):
        goes_ref[t : t + 1, :] = jnp.where(mine[:, t : t + 1] == slab_lane, 1.0, 0.0)


def message_kernel(proj_ref, out_ref, rows):
    rows[...] = jnp.zeros_like(rows)
    rows[pl.ds(0, proj_ref.shape[1]), :] = proj_ref[0].astype(F32)
    total = rows.shape[1]
    count = out_ref.shape[0]
    for b in range(count):
        moved = pltpu.roll(rows[...], (total - b * (total // count)) % total, 1)
        out_ref[b] = moved[:, :NG].astype(BF)


def streamed(out_ref, held, sems, chunk, start, size):
    part = pl.ds(start, size)
    copy = pltpu.make_async_copy(held.at[part], out_ref.at[part], sems.at[chunk])
    copy.start()
    return copy


def charge_kernel(goes_ref, proj_ref, block_ref, out_ref, held, sems):
    slab = lax.axis_index("slab")
    groups = proj_ref.shape[0]
    atoms = block_ref.shape[1] // CHANNEL_ROWS
    lane = lax.broadcasted_iota(jnp.int32, (CHANNEL_ROWS, NG), 1)
    weights = [jnp.zeros((CHANNEL_ROWS, NG), F32)] * atoms
    for b in range(groups):
        mine = pltpu.roll(proj_ref[b].astype(F32), (NG - slab * atoms) & (NG - 1), 1)
        for t in range(atoms):
            weights[t] = jnp.where(lane // SLABS == b, mine[:, t : t + 1], weights[t])
    pieces = []
    for t in range(atoms):
        behind = pltpu.roll(weights[t], NG - SLABS, 1)
        picked = weights[t] * goes_ref[t : t + 1, :]
        pieces.append(jnp.concatenate([picked * weights[t], picked * behind], axis=1))
    weight = jnp.concatenate(pieces, axis=0)
    bound = jnp.sum(jnp.abs(weight), axis=0, keepdims=True) * BLOCK_LIMIT
    weight = jnp.transpose(weight * (QMAX / jnp.maximum(bound, 1e-30)))
    both = jnp.concatenate(split(weight), axis=1)
    half = weight.shape[0] // 2
    size = half // 4
    copies = []
    blocks = [jnp.concatenate([block_ref[y], block_ref[y]], axis=0) for y in range(8)]
    for n in range(4):
        pairs = []
        for p in range(2):
            rows = both[p * half + n * size : p * half + (n + 1) * size]
            values = jnp.round(jnp.stack([dot(rows, block) for block in blocks]))
            pairs.append(jnp.swapaxes(values, 0, 1))
        held[pl.ds(n * size, size)] = to_int16(jnp.concatenate(pairs, axis=1))
        copies.append(streamed(out_ref, held, sems, n, n * size, size))
    for copy in copies:
        copy.wait()


def density_kernel(p, place_vmem, here_ref, charge_ref, own_ref, next_ref, proj_ref, next_proj_ref, right_ref, left_ref, out_ref, field, second, scales, place_ref, sem):
    fetch = pltpu.make_async_copy(place_vmem, place_ref, sem)
    fetch.start()
    rows, owners = here_ref.shape[0], charge_ref.shape[0]
    count = owners // rows
    atoms = NG // count
    own_lane = lax.broadcasted_iota(jnp.int32, (count, NG), 1) // atoms == lax.broadcasted_iota(jnp.int32, (count, NG), 0)
    sizes = jnp.sum(jnp.abs(proj_ref[0].astype(F32) * next_proj_ref[0].astype(F32)), axis=0, keepdims=True)
    for r in range(rows):
        bound = sizes[:, r * NG : (r + 1) * NG] * here_ref[r : r + 1, :]
        total = jnp.sum(jnp.where(own_lane, bound, 0.0), axis=1, keepdims=True)
        scales[pl.ds(r * count, count), :] = jnp.broadcast_to(total, (count, NG))
    for x in range(PLANES):
        field[x] = own_ref[0, x].astype(F32) * next_ref[0, x].astype(F32)
    lane = lax.broadcasted_iota(jnp.int32, (8, NG), 1)
    fetch.wait()

    second[...] = jnp.zeros_like(second)

    def tiles_of(d, place, total):
        plane = place & 15
        brick_y = (place >> 4) & 15
        shift = (place >> 8) * 8
        inside = ((lane - shift) & (NG - 1)) < 16
        tile = from_int16(charge_ref[d])[8 * p : 8 * p + 8] * scales[pl.ds(d, 1), :]
        places = []
        for g in range(8):
            turned = pltpu.roll(tile, (shift + (NG - 16 * g)) & (NG - 1), 1)
            row = pl.multiple_of(((brick_y + g % 2) & (NG // 8 - 1)) * 8, 8)
            at = (plane + g // 2, pl.ds(row, 8))
            places.append((at, total[at] + jnp.where(inside, turned, 0.0)))
        return places

    def add_row(r, carry):
        for i in range(0, count, 2):
            pair = []
            for k, total in enumerate((field, second)):
                pair.append(tiles_of(r * count + i + k, place_ref[r, (i + k) * atoms], total))
            for places, total in zip(pair, (field, second)):
                for at, value in places:
                    total[at] = value
        return carry

    lax.fori_loop(0, rows, add_row, 0)
    for x in range(0, PLANES, 2):
        both = times_right(jnp.concatenate([field[x] + second[x], field[x + 1] + second[x + 1]], axis=0), right_ref)
        both = times_left(left_ref, jnp.concatenate([both[:NG], both[NG:]], axis=1))
        field[x] = both[:, :NG]
        field[x + 1] = both[:, NG:]

    for d in range(SLABS):
        rows = pl.ds(d * ROWS, ROWS)
        largest = jnp.abs(field[0, rows])
        for x in range(1, PLANES):
            largest = jnp.maximum(largest, jnp.abs(field[x, rows]))
        code = step_code(largest)
        factor = 1.0 / step_size(code)
        lows = []
        for x in range(PLANES):
            scaled = field[x, rows] * factor
            whole = jnp.round(scaled)
            out_ref[d, x] = to_int16(whole)
            lows.append((scaled - whole)[0:1])
        out_ref[d, PLANES] = to_int16(code)
        low = jnp.concatenate(lows, axis=0) * (2.0 * QMAX)
        out_ref[d, PLANES + 1] = to_int16(jnp.round(low))


def solve_kernel(base, squares_ref, in_ref, fold_x_ref, fold_z_ref, left_ref, *rest):
    *more, out_ref, field = rest

    for s in range(SLABS):
        step = step_size(from_int16(in_ref[s, base + PLANES]))
        planes = from_int16(in_ref[s, pl.ds(base, PLANES)]) * step[None]
        low = from_int16(in_ref[s, base + PLANES + 1]) * (step[0:1] * (0.5 / QMAX))
        rows = pl.ds(ROUND[s] * PLANES, PLANES)
        field[:, rows, :] = jnp.swapaxes(planes, 0, 1)
        field[0, rows, :] = field[0, rows, :] + low
    fold = fold_x_ref[...] + fold_z_ref[...]
    squares = squares_ref[pl.ds(lax.axis_index("slab"), 1), :]
    for r in range(0, ROWS, 2):
        halves = []
        for k in range(2):
            total = fold + squares[:, r + k : r + k + 1]
            halves.append(jnp.where(total > 0, KERNEL_SCALE / (total + SCREENING_RANGE), 0.0) * (1.0 / NG**3))
        columns = jnp.concatenate([field[r], field[r + 1]], axis=1)
        spectrum = times_left(left_ref, columns) * jnp.concatenate(halves, axis=1)
        columns = times_left(left_ref, spectrum)
        field[r] = columns[:, :NG]
        field[r + 1] = columns[:, NG:]
    for s in range(SLABS):
        planes = jnp.swapaxes(field[:, pl.ds(ROUND[s] * PLANES, PLANES), :], 0, 1)
        code = step_code(jnp.max(jnp.abs(planes), axis=0))
        out_ref[s, pl.ds(0, PLANES)] = to_int16(jnp.round(planes * (1.0 / step_size(code))[None]))
        out_ref[s, PLANES] = to_int16(code)
        for more_ref in more:
            out_ref[s, pl.ds(BACK_TILES, FWD_TILES)] = more_ref[s]


def potential_pair(in_ref, steps, x, left_ref, right_ref):
    halves = []
    for k in range(2):
        halves.append(jnp.concatenate([from_int16(in_ref[s, x + k]) * steps[s] for s in range(SLABS)], axis=0))
    both = times_left(left_ref, jnp.concatenate(halves, axis=1))
    both = times_right(jnp.concatenate([both[:, :NG], both[:, NG:]], axis=0), right_ref)
    return both[:NG], both[NG:]


def back_cross_kernel(in_ref, own_ref, next_ref, left_ref, right_ref, kept_ref, sent_ref, codes):
    steps = [step_size(from_int16(in_ref[s, PLANES])) for s in range(SLABS)]
    for x in range(0, PLANES, 2):
        pair = potential_pair(in_ref, steps, x, left_ref, right_ref)
        for k in range(2):
            potential = pair[k]
            kept_ref[x + k] = potential * next_ref[0, x + k].astype(F32)
            product = potential * own_ref[0, x + k].astype(F32)
            code = step_code(jnp.max(jnp.abs(product), axis=0, keepdims=True))
            codes[x + k : x + k + 1, :] = code
            sent_ref[pl.ds((x + k) * NG, NG), :] = to_int16(jnp.round(product * (1.0 / step_size(code))))
    sent_ref[pl.ds(PLANES * NG, PLANES), :] = to_int16(codes[...])


def back_own_kernel(in_ref, own_ref, kept_ref, sent_ref, left_ref, right_ref, out_ref, held, sems):
    copies = []
    steps = [step_size(from_int16(in_ref[s, PLANES])) for s in range(SLABS)]
    sent_steps = step_size(from_int16(sent_ref[pl.ds(PLANES * NG, PLANES), :]))
    for x in range(0, PLANES, 2):
        pair = potential_pair(in_ref, steps, x, left_ref, right_ref)
        for k in range(2):
            sent = from_int16(sent_ref[pl.ds((x + k) * NG, NG), :]) * sent_steps[x + k : x + k + 1]
            held[x + k] = kept_ref[x + k] + sent + pair[k] * own_ref[0, x + k].astype(F32)
        copies.append(streamed(out_ref.at[0], held, sems, x // 2, x, 2))
    for copy in copies:
        copy.wait()


def hbm():
    return pl.BlockSpec(memory_space=pltpu.HBM)


def vmem():
    return pl.BlockSpec(memory_space=pltpu.VMEM)


def smem():
    return pl.BlockSpec(memory_space=pltpu.SMEM)


def call(kernel, in_specs, out_shape, scratch, name, micros, out_specs=None):
    many = isinstance(out_shape, (list, tuple))
    out_specs = out_specs or [vmem()] * (len(out_shape) if many else 1)
    return pl.pallas_call(
        kernel,
        in_specs=in_specs,
        out_specs=out_specs if many else out_specs[0],
        out_shape=out_shape,
        scratch_shapes=scratch,
        name=name,
        cost_estimate=pl.CostEstimate(
            flops=int(micros * 1e8), bytes_accessed=int(micros * 3.5e6), transcendentals=0
        ),
        compiler_params=pltpu.CompilerParams(vmem_limit_bytes=VMEM_LIMIT),
    )


def from_behind(block, axis, distance):
    count = lax.axis_size(axis)
    return lax.ppermute(block, axis, [((i - distance) % count, i) for i in range(count)])


def per_device(orbitals, projections, aug_blocks, atom_home):
    n_band = lax.axis_size("band")
    n_slab = lax.axis_size("slab")
    owners = n_band * n_slab
    atom_dev = aug_blocks.shape[0]
    right, left, left_y, left_y_back = (jnp.asarray(t) for t in tables())
    squares = fold_square_host()


    messages = call(
        message_kernel,
        [vmem()],
        jax.ShapeDtypeStruct((n_band, CHANNEL_ROWS, NG), BF),
        [pltpu.VMEM((CHANNEL_ROWS, projections.shape[2]), F32)],
        "messages",
        1,
    )(projections)
    all_proj = lax.all_to_all(
        messages, "band", split_axis=0, concat_axis=0, tiled=True, axis_index_groups=[list(range(n_band))]
    )

    home_rows = atom_home.shape[1] // NG
    blocks, places, here, goes = call(
        local_kernel,
        [pl.BlockSpec(memory_space=pl.ANY), hbm(), vmem()],
        [
            jax.ShapeDtypeStruct((8, atom_dev * CHANNEL_ROWS, NG), BF),
            jax.ShapeDtypeStruct((home_rows, NG), jnp.int32),
            jax.ShapeDtypeStruct((home_rows, NG), F32),
            jax.ShapeDtypeStruct((atom_dev, NG), F32),
        ],
        [pltpu.VMEM((8, atom_dev * CHANNEL_ROWS, NG), F32)] * 2
        + [pltpu.VMEM(atom_home.shape, jnp.int32), pltpu.SemaphoreType.DMA],
        "local",
        1,
    )(messages, atom_home, aug_blocks.transpose(0, 2, 1, 3))
    own, proj, blocks = lax.optimization_barrier((orbitals, projections, blocks))
    next_proj = from_behind(proj, "band", -1)
    nxt = from_behind(own, "band", -1)

    charges = call(
        charge_kernel,
        [vmem()] * 3,
        jax.ShapeDtypeStruct((owners, 16, NG), jnp.int16),
        [pltpu.VMEM((owners, 16, NG), jnp.int16), pltpu.SemaphoreType.DMA((4,))],
        "charges",
        2,
        [hbm()],
    )(goes, all_proj, blocks)
    charges = lax.all_to_all(charges, ("band", "slab"), split_axis=0, concat_axis=0, tiled=True)

    fold_y = jnp.asarray(squares[row_order()])
    fold_x = jnp.asarray(np.broadcast_to(squares[:, None], (NG, NG)).copy())
    fold_z = jnp.asarray(squares[None, :])

    def density(p, other, other_proj):
        return call(
            functools.partial(density_kernel, p),
            [vmem()] * 9,
            jax.ShapeDtypeStruct((n_slab, FWD_TILES, 16, NG), jnp.int16),
            [
                pltpu.VMEM((PLANES, NG, NG), F32),
                pltpu.VMEM((PLANES, NG, NG), F32),
                pltpu.VMEM((owners, NG), F32),
                pltpu.SMEM(places.shape, jnp.int32),
                pltpu.SemaphoreType.DMA,
            ],
            "density" + str(p),
            6,
        )(places, here, charges, own, other, proj, other_proj, right, left_y)

    def solve(name, base, spectrum, *more):
        tiles = BACK_TILES + FWD_TILES * len(more)
        return call(
            functools.partial(solve_kernel, base),
            [vmem()] * (5 + len(more)),
            jax.ShapeDtypeStruct((n_slab, tiles, 16, NG), jnp.int16),
            [pltpu.VMEM((ROWS, NG, NG), F32)],
            name,
            3,
        )(fold_y, spectrum, fold_x, fold_z, left, *more)

    def swap(block):
        return lax.all_to_all(
            block, "slab", split_axis=0, concat_axis=0, tiled=True, axis_index_groups=[list(ROUND)]
        )

    cross = swap(density(1, nxt, next_proj))
    cross = swap(solve("solve1", 0, cross, density(0, own, proj)))
    mine = swap(solve("solve0", BACK_TILES, cross))

    kept, sent = call(
        back_cross_kernel,
        [vmem()] * 5,
        [
            jax.ShapeDtypeStruct((PLANES, NG, NG), F32),
            jax.ShapeDtypeStruct((PLANES * NG + PLANES, NG), jnp.int16),
        ],
        [pltpu.VMEM((PLANES, NG), F32)],
        "back_cross",
        2,
    )(cross, own, nxt, left_y_back, right)
    got = from_behind(sent, "band", 1)
    return call(
        back_own_kernel,
        [vmem()] * 6,
        jax.ShapeDtypeStruct((1, PLANES, NG, NG), F32),
        [pltpu.VMEM((PLANES, NG, NG), F32), pltpu.SemaphoreType.DMA((PLANES // 2,))],
        "back_own",
        2,
        [hbm()],
    )(mine, own, kept, got, left_y_back, right)


def solution(mesh):
    in_specs = (
        P("band", "slab", None, None),
        P("band", None, None),
        P(("band", "slab"), None, None, None),
        P(),
    )
    out_specs = P("band", "slab", None, None)
    return jax.shard_map(
        per_device, mesh=mesh, in_specs=in_specs, out_specs=out_specs, check_vma=False
    )
```

```python
import functools
import math

import numpy as np
import jax
import jax.numpy as jnp
from jax import lax
from jax.experimental import pallas as pl
from jax.experimental.pallas import tpu as pltpu
from jax.sharding import PartitionSpec as P

KERNEL_SCALE = 0.5
SCREENING_RANGE = 0.002
NG = 128
SLABS = 8
ROWS = NG // SLABS
PLANES = NG // SLABS
BLOCK_LIMIT = 3.0
QMAX = 32760.0
STEPS = 8.0
CHANNEL_ROWS = 16
ROUND = (0, 1, 2, 3, 4, 5, 6, 7)
FWD_TILES = PLANES + 2
BACK_TILES = PLANES + 1
BF = jnp.bfloat16
F32 = jnp.float32
VMEM_LIMIT = 50 * 1024 * 1024


def hartley_host():
    index = np.arange(NG)
    angle = (index[:, None] * index[None, :] % NG) * (2.0 * math.pi / NG)
    return (np.cos(angle) + np.sin(angle)).astype(np.float32)


def split_host(table):
    high = table.astype(jnp.bfloat16)
    low = (table - high.astype(np.float32)).astype(jnp.bfloat16)
    return high, low


def row_order():
    by_size = sorted(range(NG), key=lambda k: (min(k, NG - k), k))
    return np.array([[by_size[d + SLABS * r] for r in range(ROWS)] for d in range(SLABS)])


def fold_square_host():
    index = np.arange(NG)
    return ((np.minimum(index, NG - index)).astype(np.float32) * np.float32(2.0 * math.pi / NG)) ** 2


def tables():
    table = hartley_host()
    high, low = split_host(table)
    order = row_order()[list(ROUND)].reshape(-1)
    high_y, low_y = high[order], low[order]
    top = np.concatenate([high, low], axis=1)
    bottom = np.concatenate([high, np.zeros_like(high)], axis=1)
    right = np.concatenate([top, bottom], axis=0)
    left = np.concatenate([high, low, high], axis=1)
    left_y = np.concatenate([high_y, low_y, high_y], axis=1)
    left_y_back = np.concatenate([high_y.T, low_y.T, high_y.T], axis=1)
    return right, left, left_y, left_y_back


def split(value):
    high = value.astype(BF)
    low = (value - high.astype(F32)).astype(BF)
    return high, low


def dot(a, b):
    return jnp.dot(a, b, preferred_element_type=F32)


def times_right(value, right_ref):
    high, low = split(value)
    both = dot(jnp.concatenate([high, low], axis=1), right_ref[...])
    return both[:, :NG] + both[:, NG:]


def times_left(left_ref, value):
    high, low = split(value)
    return dot(left_ref[...], jnp.concatenate([high, high, low], axis=0))


def step_code(largest):
    return jnp.ceil(jnp.log(jnp.maximum(largest, 1e-30)) * (STEPS / math.log(2.0)))


def step_size(code):
    return jnp.exp(code * (math.log(2.0) / STEPS)) * (1.001 / QMAX)


def to_int16(value):
    return value.astype(jnp.int32).astype(jnp.int16)


def from_int16(value):
    return value.astype(jnp.int32).astype(F32)


def local_kernel(after_ref, home_any, block_ref, out_ref, place_ref, here_ref, goes_ref, rows, turned, home_ref, sem):
    fetch = pltpu.make_async_copy(home_any, home_ref, sem)
    fetch.start()
    lane = lax.broadcasted_iota(jnp.int32, (1, NG), 1) // 8
    atoms, channels, bricks = block_ref.shape[:3]
    rows[...] = jnp.zeros_like(rows)
    for t in range(atoms):
        rows[:, pl.ds(CHANNEL_ROWS * t, channels), :] = jnp.swapaxes(block_ref[t].astype(F32), 0, 1)
    for k in range(bricks):
        values = rows[k]
        first = (k // 4) * 8 + (k // 2 % 2) * 2 + k % 2
        for back in range(12):
            moved = pltpu.roll(values, (first - back) % 16 * 8, 1)
            for x in range(2):
                y = back - 4 * x
                if 0 <= y < 8:
                    inside = lane == first + 4 * x
                    turned[y] = moved if k == 0 and x == 0 else jnp.where(inside, moved, turned[y])
    out_ref[...] = turned[...].astype(BF)
    fetch.wait()
    half = PLANES // 2
    slab = lax.axis_index("slab")
    here = home_ref[0:1, :] // half == slab
    place = (home_ref[0:1, :] - slab * half) * 2 + 16 * home_ref[1:2, :] + 256 * home_ref[2:3, :]
    place = jnp.where(here, place, 0)
    here = jnp.where(here, BLOCK_LIMIT / QMAX, 0.0)
    for r in range(place_ref.shape[0]):
        part = place[:, r * NG : (r + 1) * NG]
        total = part
        for t in range(1, atoms):
            total = total + pltpu.roll(part, NG - t, 1)
        place_ref[r : r + 1, :] = total
        here_ref[r : r + 1, :] = here[:, r * NG : (r + 1) * NG]
    owner = lax.axis_index("band") * SLABS + slab
    wide = home_ref.shape[1]
    mine = pltpu.roll(home_ref[0:1, :] // half, (wide - owner * atoms) & (wide - 1), 1)[:, :NG]
    slab_lane = lax.broadcasted_iota(jnp.int32, (1, NG), 1) & (SLABS - 1)
    for t in range(atoms):
        goes_ref[t : t + 1, :] = jnp.where(mine[:, t : t + 1] == slab_lane, 1.0, 0.0)


def message_kernel(proj_ref, out_ref, rows):
    rows[...] = jnp.zeros_like(rows)
    rows[pl.ds(0, proj_ref.shape[1]), :] = proj_ref[0].astype(F32)
    total = rows.shape[1]
    count = out_ref.shape[0]
    for b in range(count):
        moved = pltpu.roll(rows[...], (total - b * (total // count)) % total, 1)
        out_ref[b] = moved[:, :NG].astype(BF)


def streamed(out_ref, held, sems, chunk, start, size):
    part = pl.ds(start, size)
    copy = pltpu.make_async_copy(held.at[part], out_ref.at[part], sems.at[chunk])
    copy.start()
    return copy


def charge_kernel(goes_ref, proj_ref, block_ref, out_ref, held, sems):
    slab = lax.axis_index("slab")
    groups = proj_ref.shape[0]
    atoms = block_ref.shape[1] // CHANNEL_ROWS
    lane = lax.broadcasted_iota(jnp.int32, (CHANNEL_ROWS, NG), 1)
    weights = [jnp.zeros((CHANNEL_ROWS, NG), F32)] * atoms
    for b in range(groups):
        mine = pltpu.roll(proj_ref[b].astype(F32), (NG - slab * atoms) & (NG - 1), 1)
        for t in range(atoms):
            weights[t] = jnp.where(lane // SLABS == b, mine[:, t : t + 1], weights[t])
    pieces = []
    for t in range(atoms):
        behind = pltpu.roll(weights[t], SLABS, 1)
        picked = weights[t] * goes_ref[t : t + 1, :]
        pieces.append(jnp.concatenate([picked * weights[t], picked * behind], axis=1))
    weight = jnp.concatenate(pieces, axis=0)
    bound = jnp.sum(jnp.abs(weight), axis=0, keepdims=True) * BLOCK_LIMIT
    weight = jnp.transpose(weight * (QMAX / jnp.maximum(bound, 1e-30)))
    both = jnp.concatenate(split(weight), axis=1)
    half = weight.shape[0] // 2
    size = half // 4
    copies = []
    blocks = [jnp.concatenate([block_ref[y], block_ref[y]], axis=0) for y in range(8)]
    for n in range(4):
        pairs = []
        for p in range(2):
            rows = both[p * half + n * size : p * half + (n + 1) * size]
            values = jnp.round(jnp.stack([dot(rows, block) for block in blocks]))
            pairs.append(jnp.swapaxes(values, 0, 1))
        held[pl.ds(n * size, size)] = to_int16(jnp.concatenate(pairs, axis=1))
        copies.append(streamed(out_ref, held, sems, n, n * size, size))
    for copy in copies:
        copy.wait()


def density_kernel(p, place_vmem, here_ref, charge_ref, own_ref, prev_ref, proj_ref, prev_proj_ref, right_ref, left_ref, out_ref, field, second, scales, place_ref, sem):
    fetch = pltpu.make_async_copy(place_vmem, place_ref, sem)
    fetch.start()
    rows, owners = here_ref.shape[0], charge_ref.shape[0]
    count = owners // rows
    atoms = NG // count
    own_lane = lax.broadcasted_iota(jnp.int32, (count, NG), 1) // atoms == lax.broadcasted_iota(jnp.int32, (count, NG), 0)
    sizes = jnp.sum(jnp.abs(proj_ref[0].astype(F32) * prev_proj_ref[0].astype(F32)), axis=0, keepdims=True)
    for r in range(rows):
        bound = sizes[:, r * NG : (r + 1) * NG] * here_ref[r : r + 1, :]
        total = jnp.sum(jnp.where(own_lane, bound, 0.0), axis=1, keepdims=True)
        scales[pl.ds(r * count, count), :] = jnp.broadcast_to(total, (count, NG))
    for x in range(PLANES):
        field[x] = own_ref[0, x].astype(F32) * prev_ref[0, x].astype(F32)
    lane = lax.broadcasted_iota(jnp.int32, (8, NG), 1)
    fetch.wait()

    second[...] = jnp.zeros_like(second)

    def tiles_of(d, place, total):
        plane = place & 15
        brick_y = (place >> 4) & 15
        shift = (place >> 8) * 8
        inside = ((lane - shift) & (NG - 1)) < 16
        tile = from_int16(charge_ref[d])[8 * p : 8 * p + 8] * scales[pl.ds(d, 1), :]
        places = []
        for g in range(8):
            turned = pltpu.roll(tile, (shift + (NG - 16 * g)) & (NG - 1), 1)
            row = pl.multiple_of(((brick_y + g % 2) & (NG // 8 - 1)) * 8, 8)
            at = (plane + g // 2, pl.ds(row, 8))
            places.append((at, total[at] + jnp.where(inside, turned, 0.0)))
        return places

    def add_row(r, carry):
        for i in range(0, count, 2):
            pair = []
            for k, total in enumerate((field, second)):
                pair.append(tiles_of(r * count + i + k, place_ref[r, (i + k) * atoms], total))
            for places, total in zip(pair, (field, second)):
                for at, value in places:
                    total[at] = value
        return carry

    lax.fori_loop(0, rows, add_row, 0)
    for x in range(0, PLANES, 2):
        both = times_right(jnp.concatenate([field[x] + second[x], field[x + 1] + second[x + 1]], axis=0), right_ref)
        both = times_left(left_ref, jnp.concatenate([both[:NG], both[NG:]], axis=1))
        field[x] = both[:, :NG]
        field[x + 1] = both[:, NG:]

    for d in range(SLABS):
        rows = pl.ds(d * ROWS, ROWS)
        largest = jnp.abs(field[0, rows])
        for x in range(1, PLANES):
            largest = jnp.maximum(largest, jnp.abs(field[x, rows]))
        code = step_code(largest)
        factor = 1.0 / step_size(code)
        lows = []
        for x in range(PLANES):
            scaled = field[x, rows] * factor
            whole = jnp.round(scaled)
            out_ref[d, x] = to_int16(whole)
            lows.append((scaled - whole)[0:1])
        out_ref[d, PLANES] = to_int16(code)
        low = jnp.concatenate(lows, axis=0) * (2.0 * QMAX)
        out_ref[d, PLANES + 1] = to_int16(jnp.round(low))


def solve_kernel(base, squares_ref, in_ref, fold_x_ref, fold_z_ref, left_ref, *rest):
    *more, out_ref, field = rest

    for s in range(SLABS):
        step = step_size(from_int16(in_ref[s, base + PLANES]))
        planes = from_int16(in_ref[s, pl.ds(base, PLANES)]) * step[None]
        low = from_int16(in_ref[s, base + PLANES + 1]) * (step[0:1] * (0.5 / QMAX))
        rows = pl.ds(ROUND[s] * PLANES, PLANES)
        field[:, rows, :] = jnp.swapaxes(planes, 0, 1)
        field[0, rows, :] = field[0, rows, :] + low
    fold = fold_x_ref[...] + fold_z_ref[...]
    squares = squares_ref[pl.ds(lax.axis_index("slab"), 1), :]
    for r in range(0, ROWS, 2):
        halves = []
        for k in range(2):
            total = fold + squares[:, r + k : r + k + 1]
            halves.append(jnp.where(total > 0, KERNEL_SCALE / (total + SCREENING_RANGE), 0.0) * (1.0 / NG**3))
        columns = jnp.concatenate([field[r], field[r + 1]], axis=1)
        spectrum = times_left(left_ref, columns) * jnp.concatenate(halves, axis=1)
        columns = times_left(left_ref, spectrum)
        field[r] = columns[:, :NG]
        field[r + 1] = columns[:, NG:]
    for s in range(SLABS):
        planes = jnp.swapaxes(field[:, pl.ds(ROUND[s] * PLANES, PLANES), :], 0, 1)
        code = step_code(jnp.max(jnp.abs(planes), axis=0))
        out_ref[s, pl.ds(0, PLANES)] = to_int16(jnp.round(planes * (1.0 / step_size(code))[None]))
        out_ref[s, PLANES] = to_int16(code)
        for more_ref in more:
            out_ref[s, pl.ds(BACK_TILES, FWD_TILES)] = more_ref[s]


def potential_pair(in_ref, steps, x, left_ref, right_ref):
    halves = []
    for k in range(2):
        halves.append(jnp.concatenate([from_int16(in_ref[s, x + k]) * steps[s] for s in range(SLABS)], axis=0))
    both = times_left(left_ref, jnp.concatenate(halves, axis=1))
    both = times_right(jnp.concatenate([both[:, :NG], both[:, NG:]], axis=0), right_ref)
    return both[:NG], both[NG:]


def back_cross_kernel(in_ref, own_ref, prev_ref, left_ref, right_ref, kept_ref, sent_ref, codes):
    steps = [step_size(from_int16(in_ref[s, PLANES])) for s in range(SLABS)]
    for x in range(0, PLANES, 2):
        pair = potential_pair(in_ref, steps, x, left_ref, right_ref)
        for k in range(2):
            potential = pair[k]
            kept_ref[x + k] = potential * prev_ref[0, x + k].astype(F32)
            product = potential * own_ref[0, x + k].astype(F32)
            code = step_code(jnp.max(jnp.abs(product), axis=0, keepdims=True))
            codes[x + k : x + k + 1, :] = code
            sent_ref[pl.ds((x + k) * NG, NG), :] = to_int16(jnp.round(product * (1.0 / step_size(code))))
    sent_ref[pl.ds(PLANES * NG, PLANES), :] = to_int16(codes[...])


def back_own_kernel(in_ref, own_ref, kept_ref, sent_ref, left_ref, right_ref, out_ref, held, sems):
    copies = []
    steps = [step_size(from_int16(in_ref[s, PLANES])) for s in range(SLABS)]
    sent_steps = step_size(from_int16(sent_ref[pl.ds(PLANES * NG, PLANES), :]))
    for x in range(0, PLANES, 2):
        pair = potential_pair(in_ref, steps, x, left_ref, right_ref)
        for k in range(2):
            sent = from_int16(sent_ref[pl.ds((x + k) * NG, NG), :]) * sent_steps[x + k : x + k + 1]
            held[x + k] = kept_ref[x + k] + sent + pair[k] * own_ref[0, x + k].astype(F32)
        copies.append(streamed(out_ref.at[0], held, sems, x // 2, x, 2))
    for copy in copies:
        copy.wait()


def hbm():
    return pl.BlockSpec(memory_space=pltpu.HBM)


def vmem():
    return pl.BlockSpec(memory_space=pltpu.VMEM)


def smem():
    return pl.BlockSpec(memory_space=pltpu.SMEM)


def call(kernel, in_specs, out_shape, scratch, name, micros, out_specs=None):
    many = isinstance(out_shape, (list, tuple))
    out_specs = out_specs or [vmem()] * (len(out_shape) if many else 1)
    return pl.pallas_call(
        kernel,
        in_specs=in_specs,
        out_specs=out_specs if many else out_specs[0],
        out_shape=out_shape,
        scratch_shapes=scratch,
        name=name,
        cost_estimate=pl.CostEstimate(
            flops=int(micros * 1e8), bytes_accessed=int(micros * 3.5e6), transcendentals=0
        ),
        compiler_params=pltpu.CompilerParams(vmem_limit_bytes=VMEM_LIMIT),
    )


def from_behind(block, axis, distance):
    count = lax.axis_size(axis)
    return lax.ppermute(block, axis, [((i - distance) % count, i) for i in range(count)])


def per_device(orbitals, projections, aug_blocks, atom_home):
    n_band = lax.axis_size("band")
    n_slab = lax.axis_size("slab")
    owners = n_band * n_slab
    atom_dev = aug_blocks.shape[0]
    right, left, left_y, left_y_back = (jnp.asarray(t) for t in tables())
    squares = fold_square_host()


    messages = call(
        message_kernel,
        [vmem()],
        jax.ShapeDtypeStruct((n_band, CHANNEL_ROWS, NG), BF),
        [pltpu.VMEM((CHANNEL_ROWS, projections.shape[2]), F32)],
        "messages",
        1,
    )(projections)
    all_proj = lax.all_to_all(
        messages, "band", split_axis=0, concat_axis=0, tiled=True, axis_index_groups=[list(range(n_band))]
    )

    home_rows = atom_home.shape[1] // NG
    blocks, places, here, goes = call(
        local_kernel,
        [pl.BlockSpec(memory_space=pl.ANY), hbm(), vmem()],
        [
            jax.ShapeDtypeStruct((8, atom_dev * CHANNEL_ROWS, NG), BF),
            jax.ShapeDtypeStruct((home_rows, NG), jnp.int32),
            jax.ShapeDtypeStruct((home_rows, NG), F32),
            jax.ShapeDtypeStruct((atom_dev, NG), F32),
        ],
        [pltpu.VMEM((8, atom_dev * CHANNEL_ROWS, NG), F32)] * 2
        + [pltpu.VMEM(atom_home.shape, jnp.int32), pltpu.SemaphoreType.DMA],
        "local",
        1,
    )(messages, atom_home, aug_blocks.transpose(0, 2, 1, 3))
    own = orbitals
    proj, blocks = lax.optimization_barrier((projections, blocks))
    prev_proj = from_behind(proj, "band", 1)
    prev = from_behind(own, "band", 1)

    charges = call(
        charge_kernel,
        [vmem()] * 3,
        jax.ShapeDtypeStruct((owners, 16, NG), jnp.int16),
        [pltpu.VMEM((owners, 16, NG), jnp.int16), pltpu.SemaphoreType.DMA((4,))],
        "charges",
        2,
        [hbm()],
    )(goes, all_proj, blocks)
    charges = lax.all_to_all(charges, ("band", "slab"), split_axis=0, concat_axis=0, tiled=True)

    fold_y = jnp.asarray(squares[row_order()])
    fold_x = jnp.asarray(np.broadcast_to(squares[:, None], (NG, NG)).copy())
    fold_z = jnp.asarray(squares[None, :])

    def density(p, other, other_proj):
        return call(
            functools.partial(density_kernel, p),
            [vmem()] * 9,
            jax.ShapeDtypeStruct((n_slab, FWD_TILES, 16, NG), jnp.int16),
            [
                pltpu.VMEM((PLANES, NG, NG), F32),
                pltpu.VMEM((PLANES, NG, NG), F32),
                pltpu.VMEM((owners, NG), F32),
                pltpu.SMEM(places.shape, jnp.int32),
                pltpu.SemaphoreType.DMA,
            ],
            "density" + str(p),
            6,
        )(places, here, charges, own, other, proj, other_proj, right, left_y)

    def solve(name, base, spectrum, *more):
        tiles = BACK_TILES + FWD_TILES * len(more)
        return call(
            functools.partial(solve_kernel, base),
            [vmem()] * (5 + len(more)),
            jax.ShapeDtypeStruct((n_slab, tiles, 16, NG), jnp.int16),
            [pltpu.VMEM((ROWS, NG, NG), F32)],
            name,
            3,
        )(fold_y, spectrum, fold_x, fold_z, left, *more)

    def swap(block):
        return lax.all_to_all(
            block, "slab", split_axis=0, concat_axis=0, tiled=True, axis_index_groups=[list(ROUND)]
        )

    cross = swap(density(1, prev, prev_proj))
    cross = swap(solve("solve1", 0, cross, density(0, own, proj)))
    mine = swap(solve("solve0", BACK_TILES, cross))

    kept, sent = call(
        back_cross_kernel,
        [vmem()] * 5,
        [
            jax.ShapeDtypeStruct((PLANES, NG, NG), F32),
            jax.ShapeDtypeStruct((PLANES * NG + PLANES, NG), jnp.int16),
        ],
        [pltpu.VMEM((PLANES, NG), F32)],
        "back_cross",
        2,
    )(cross, own, prev, left_y_back, right)
    got = from_behind(sent, "band", -1)
    return call(
        back_own_kernel,
        [vmem()] * 6,
        jax.ShapeDtypeStruct((1, PLANES, NG, NG), F32),
        [pltpu.VMEM((PLANES, NG, NG), F32), pltpu.SemaphoreType.DMA((PLANES // 2,))],
        "back_own",
        2,
        [hbm()],
    )(mine, own, kept, got, left_y_back, right)


def solution(mesh):
    in_specs = (
        P("band", "slab", None, None),
        P("band", None, None),
        P(("band", "slab"), None, None, None),
        P(),
    )
    out_specs = P("band", "slab", None, None)
    return jax.shard_map(
        per_device, mesh=mesh, in_specs=in_specs, out_specs=out_specs, check_vma=False
    )
```

```python
import functools
import math

import numpy as np
import jax
import jax.numpy as jnp
from jax import lax
from jax.experimental import pallas as pl
from jax.experimental.pallas import tpu as pltpu
from jax.sharding import PartitionSpec as P

KERNEL_SCALE = 0.5
SCREENING_RANGE = 0.002
NG = 128
SLABS = 8
ROWS = NG // SLABS
PLANES = NG // SLABS
BLOCK_LIMIT = 3.0
QMAX = 32760.0
STEPS = 8.0
CHANNEL_ROWS = 16
ROUND = (0, 1, 2, 3, 4, 5, 6, 7)
FWD_TILES = PLANES + 2
BACK_TILES = PLANES + 1
BF = jnp.bfloat16
F32 = jnp.float32
VMEM_LIMIT = 50 * 1024 * 1024


def hartley_host():
    index = np.arange(NG)
    angle = (index[:, None] * index[None, :] % NG) * (2.0 * math.pi / NG)
    return (np.cos(angle) + np.sin(angle)).astype(np.float32)


def split_host(table):
    high = table.astype(jnp.bfloat16)
    low = (table - high.astype(np.float32)).astype(jnp.bfloat16)
    return high, low


def row_order():
    by_size = sorted(range(NG), key=lambda k: (min(k, NG - k), k))
    return np.array([[by_size[d + SLABS * r] for r in range(ROWS)] for d in range(SLABS)])


def fold_square_host():
    index = np.arange(NG)
    return ((np.minimum(index, NG - index)).astype(np.float32) * np.float32(2.0 * math.pi / NG)) ** 2


def tables():
    table = hartley_host()
    high, low = split_host(table)
    order = row_order()[list(ROUND)].reshape(-1)
    high_y, low_y = high[order], low[order]
    top = np.concatenate([high, low], axis=1)
    bottom = np.concatenate([high, np.zeros_like(high)], axis=1)
    right = np.concatenate([top, bottom], axis=0)
    left = np.concatenate([high, low, high], axis=1)
    left_y = np.concatenate([high_y, low_y, high_y], axis=1)
    left_y_back = np.concatenate([high_y.T, low_y.T, high_y.T], axis=1)
    return right, left, left_y, left_y_back


def split(value):
    high = value.astype(BF)
    low = (value - high.astype(F32)).astype(BF)
    return high, low


def dot(a, b):
    return jnp.dot(a, b, preferred_element_type=F32)


def times_right(value, right_ref):
    high, low = split(value)
    both = dot(jnp.concatenate([high, low], axis=1), right_ref[...])
    return both[:, :NG] + both[:, NG:]


def times_left(left_ref, value):
    high, low = split(value)
    return dot(left_ref[...], jnp.concatenate([high, high, low], axis=0))


def step_code(largest):
    return jnp.ceil(jnp.log(jnp.maximum(largest, 1e-30)) * (STEPS / math.log(2.0)))


def step_size(code):
    return jnp.exp(code * (math.log(2.0) / STEPS)) * (1.001 / QMAX)


def to_int16(value):
    return value.astype(jnp.int32).astype(jnp.int16)


def from_int16(value):
    return value.astype(jnp.int32).astype(F32)


def local_kernel(after_ref, home_any, block_ref, out_ref, place_ref, here_ref, goes_ref, rows, turned, home_ref, sem):
    fetch = pltpu.make_async_copy(home_any, home_ref, sem)
    fetch.start()
    lane = lax.broadcasted_iota(jnp.int32, (1, NG), 1) // 8
    atoms, channels, bricks = block_ref.shape[:3]
    rows[...] = jnp.zeros_like(rows)
    for t in range(atoms):
        rows[:, pl.ds(CHANNEL_ROWS * t, channels), :] = jnp.swapaxes(block_ref[t].astype(F32), 0, 1)
    for k in range(bricks):
        values = rows[k]
        first = (k // 4) * 8 + (k // 2 % 2) * 2 + k % 2
        for back in range(12):
            moved = pltpu.roll(values, (first - back) % 16 * 8, 1)
            for x in range(2):
                y = back - 4 * x
                if 0 <= y < 8:
                    inside = lane == first + 4 * x
                    turned[y] = moved if k == 0 and x == 0 else jnp.where(inside, moved, turned[y])
    out_ref[...] = turned[...].astype(BF)
    fetch.wait()
    half = PLANES // 2
    slab = lax.axis_index("slab")
    here = home_ref[0:1, :] // half == slab
    place = (home_ref[0:1, :] - slab * half) * 2 + 16 * home_ref[1:2, :] + 256 * home_ref[2:3, :]
    place = jnp.where(here, place, 0)
    here = jnp.where(here, BLOCK_LIMIT / QMAX, 0.0)
    for r in range(place_ref.shape[0]):
        part = place[:, r * NG : (r + 1) * NG]
        total = part
        for t in range(1, atoms):
            total = total + pltpu.roll(part, NG - t, 1)
        place_ref[r : r + 1, :] = total
        here_ref[r : r + 1, :] = here[:, r * NG : (r + 1) * NG]
    owner = lax.axis_index("band") * SLABS + slab
    wide = home_ref.shape[1]
    mine = pltpu.roll(home_ref[0:1, :] // half, (wide - owner * atoms) & (wide - 1), 1)[:, :NG]
    slab_lane = lax.broadcasted_iota(jnp.int32, (1, NG), 1) & (SLABS - 1)
    for t in range(atoms):
        goes_ref[t : t + 1, :] = jnp.where(mine[:, t : t + 1] == slab_lane, 1.0, 0.0)


def message_kernel(proj_ref, out_ref, rows):
    rows[...] = jnp.zeros_like(rows)
    rows[pl.ds(0, proj_ref.shape[1]), :] = proj_ref[0].astype(F32)
    total = rows.shape[1]
    count = out_ref.shape[0]
    for b in range(count):
        moved = pltpu.roll(rows[...], (total - b * (total // count)) % total, 1)
        out_ref[b] = moved[:, :NG].astype(BF)


def streamed(out_ref, held, sems, chunk, start, size):
    part = pl.ds(start, size)
    copy = pltpu.make_async_copy(held.at[part], out_ref.at[part], sems.at[chunk])
    copy.start()
    return copy


def charge_kernel(goes_ref, proj_ref, block_ref, out_ref, held, sems):
    slab = lax.axis_index("slab")
    groups = proj_ref.shape[0]
    atoms = block_ref.shape[1] // CHANNEL_ROWS
    lane = lax.broadcasted_iota(jnp.int32, (CHANNEL_ROWS, NG), 1)
    weights = [jnp.zeros((CHANNEL_ROWS, NG), F32)] * atoms
    for b in range(groups):
        mine = pltpu.roll(proj_ref[b].astype(F32), (NG - slab * atoms) & (NG - 1), 1)
        for t in range(atoms):
            weights[t] = jnp.where(lane // SLABS == b, mine[:, t : t + 1], weights[t])
    pieces = []
    for t in range(atoms):
        behind = pltpu.roll(weights[t], SLABS, 1)
        picked = weights[t] * goes_ref[t : t + 1, :]
        pieces.append(jnp.concatenate([picked * weights[t], picked * behind], axis=1))
    weight = jnp.concatenate(pieces, axis=0)
    bound = jnp.sum(jnp.abs(weight), axis=0, keepdims=True) * BLOCK_LIMIT
    weight = jnp.transpose(weight * (QMAX / jnp.maximum(bound, 1e-30)))
    both = jnp.concatenate(split(weight), axis=1)
    half = weight.shape[0] // 2
    size = half // 4
    copies = []
    blocks = [jnp.concatenate([block_ref[y], block_ref[y]], axis=0) for y in range(8)]
    for n in range(4):
        pairs = []
        for p in range(2):
            rows = both[p * half + n * size : p * half + (n + 1) * size]
            values = jnp.round(jnp.stack([dot(rows, block) for block in blocks]))
            pairs.append(jnp.swapaxes(values, 0, 1))
        held[pl.ds(n * size, size)] = to_int16(jnp.concatenate(pairs, axis=1))
        copies.append(streamed(out_ref, held, sems, n, n * size, size))
    for copy in copies:
        copy.wait()


def density_kernel(p, place_vmem, here_ref, charge_ref, own_ref, prev_ref, proj_ref, prev_proj_ref, right_ref, left_ref, out_ref, field, second, scales, place_ref, sem):
    fetch = pltpu.make_async_copy(place_vmem, place_ref, sem)
    fetch.start()
    rows, owners = here_ref.shape[0], charge_ref.shape[0]
    count = owners // rows
    atoms = NG // count
    own_lane = lax.broadcasted_iota(jnp.int32, (count, NG), 1) // atoms == lax.broadcasted_iota(jnp.int32, (count, NG), 0)
    sizes = jnp.sum(jnp.abs(proj_ref[0].astype(F32) * prev_proj_ref[0].astype(F32)), axis=0, keepdims=True)
    for r in range(rows):
        bound = sizes[:, r * NG : (r + 1) * NG] * here_ref[r : r + 1, :]
        total = jnp.sum(jnp.where(own_lane, bound, 0.0), axis=1, keepdims=True)
        scales[pl.ds(r * count, count), :] = jnp.broadcast_to(total, (count, NG))
    for x in range(PLANES):
        field[x] = own_ref[0, x].astype(F32) * prev_ref[0, x].astype(F32)
    lane = lax.broadcasted_iota(jnp.int32, (8, NG), 1)
    fetch.wait()

    second[...] = jnp.zeros_like(second)

    def tiles_of(d, place, total):
        plane = place & 15
        brick_y = (place >> 4) & 15
        shift = (place >> 8) * 8
        inside = ((lane - shift) & (NG - 1)) < 16
        tile = from_int16(charge_ref[d])[8 * p : 8 * p + 8] * scales[pl.ds(d, 1), :]
        places = []
        for g in range(8):
            turned = pltpu.roll(tile, (shift + (NG - 16 * g)) & (NG - 1), 1)
            row = pl.multiple_of(((brick_y + g % 2) & (NG // 8 - 1)) * 8, 8)
            at = (plane + g // 2, pl.ds(row, 8))
            places.append((at, total[at] + jnp.where(inside, turned, 0.0)))
        return places

    def add_row(r, carry):
        for i in range(0, count, 2):
            pair = []
            for k, total in enumerate((field, second)):
                pair.append(tiles_of(r * count + i + k, place_ref[r, (i + k) * atoms], total))
            for places, total in zip(pair, (field, second)):
                for at, value in places:
                    total[at] = value
        return carry

    lax.fori_loop(0, rows, add_row, 0)
    for x in range(0, PLANES, 2):
        both = times_right(jnp.concatenate([field[x] + second[x], field[x + 1] + second[x + 1]], axis=0), right_ref)
        both = times_left(left_ref, jnp.concatenate([both[:NG], both[NG:]], axis=1))
        field[x] = both[:, :NG]
        field[x + 1] = both[:, NG:]

    for d in range(SLABS):
        rows = pl.ds(d * ROWS, ROWS)
        largest = jnp.abs(field[0, rows])
        for x in range(1, PLANES):
            largest = jnp.maximum(largest, jnp.abs(field[x, rows]))
        code = step_code(largest)
        factor = 1.0 / step_size(code)
        lows = []
        for x in range(PLANES):
            scaled = field[x, rows] * factor
            whole = jnp.round(scaled)
            out_ref[d, x] = to_int16(whole)
            lows.append((scaled - whole)[0:1])
        out_ref[d, PLANES] = to_int16(code)
        low = jnp.concatenate(lows, axis=0) * (2.0 * QMAX)
        out_ref[d, PLANES + 1] = to_int16(jnp.round(low))


def table_kernel(after_ref, squares_ref, fold_x_ref, fold_z_ref, out_ref):
    squares = squares_ref[pl.ds(lax.axis_index("slab"), 1), :]
    fold = fold_x_ref[...] + fold_z_ref[...]
    for r in range(ROWS):
        total = fold + squares[:, r : r + 1]
        out_ref[r] = jnp.where(total > 0, KERNEL_SCALE / (total + SCREENING_RANGE), 0.0) * (1.0 / NG**3)


def solve_kernel(base, in_ref, table_ref, left_ref, *rest):
    *more, out_ref, field = rest

    for s in range(SLABS):
        step = step_size(from_int16(in_ref[s, base + PLANES]))
        planes = from_int16(in_ref[s, pl.ds(base, PLANES)]) * step[None]
        low = from_int16(in_ref[s, base + PLANES + 1]) * (step[0:1] * (0.5 / QMAX))
        rows = pl.ds(ROUND[s] * PLANES, PLANES)
        field[:, rows, :] = jnp.swapaxes(planes, 0, 1)
        field[0, rows, :] = field[0, rows, :] + low
    for r in range(0, ROWS, 2):
        columns = jnp.concatenate([field[r], field[r + 1]], axis=1)
        spectrum = times_left(left_ref, columns) * jnp.concatenate([table_ref[r], table_ref[r + 1]], axis=1)
        columns = times_left(left_ref, spectrum)
        field[r] = columns[:, :NG]
        field[r + 1] = columns[:, NG:]
    for s in range(SLABS):
        planes = jnp.swapaxes(field[:, pl.ds(ROUND[s] * PLANES, PLANES), :], 0, 1)
        code = step_code(jnp.max(jnp.abs(planes), axis=0))
        out_ref[s, pl.ds(0, PLANES)] = to_int16(jnp.round(planes * (1.0 / step_size(code))[None]))
        out_ref[s, PLANES] = to_int16(code)
        for more_ref in more:
            out_ref[s, pl.ds(BACK_TILES, FWD_TILES)] = more_ref[s]


def potential_pair(in_ref, steps, x, left_ref, right_ref):
    halves = []
    for k in range(2):
        halves.append(jnp.concatenate([from_int16(in_ref[s, x + k]) * steps[s] for s in range(SLABS)], axis=0))
    both = times_left(left_ref, jnp.concatenate(halves, axis=1))
    both = times_right(jnp.concatenate([both[:, :NG], both[:, NG:]], axis=0), right_ref)
    return both[:NG], both[NG:]


def back_cross_kernel(in_ref, own_ref, prev_ref, left_ref, right_ref, kept_ref, sent_ref, codes):
    steps = [step_size(from_int16(in_ref[s, PLANES])) for s in range(SLABS)]
    for x in range(0, PLANES, 2):
        pair = potential_pair(in_ref, steps, x, left_ref, right_ref)
        for k in range(2):
            potential = pair[k]
            kept_ref[x + k] = potential * prev_ref[0, x + k].astype(F32)
            product = potential * own_ref[0, x + k].astype(F32)
            code = step_code(jnp.max(jnp.abs(product), axis=0, keepdims=True))
            codes[x + k : x + k + 1, :] = code
            sent_ref[pl.ds((x + k) * NG, NG), :] = to_int16(jnp.round(product * (1.0 / step_size(code))))
    sent_ref[pl.ds(PLANES * NG, PLANES), :] = to_int16(codes[...])


def back_own_kernel(in_ref, own_ref, kept_ref, sent_ref, left_ref, right_ref, out_ref, held, sems):
    copies = []
    steps = [step_size(from_int16(in_ref[s, PLANES])) for s in range(SLABS)]
    sent_steps = step_size(from_int16(sent_ref[pl.ds(PLANES * NG, PLANES), :]))
    for x in range(0, PLANES, 2):
        pair = potential_pair(in_ref, steps, x, left_ref, right_ref)
        for k in range(2):
            sent = from_int16(sent_ref[pl.ds((x + k) * NG, NG), :]) * sent_steps[x + k : x + k + 1]
            held[x + k] = kept_ref[x + k] + sent + pair[k] * own_ref[0, x + k].astype(F32)
        copies.append(streamed(out_ref.at[0], held, sems, x // 2, x, 2))
    for copy in copies:
        copy.wait()


def hbm():
    return pl.BlockSpec(memory_space=pltpu.HBM)


def vmem():
    return pl.BlockSpec(memory_space=pltpu.VMEM)


def smem():
    return pl.BlockSpec(memory_space=pltpu.SMEM)


def call(kernel, in_specs, out_shape, scratch, name, micros, out_specs=None):
    many = isinstance(out_shape, (list, tuple))
    out_specs = out_specs or [vmem()] * (len(out_shape) if many else 1)
    return pl.pallas_call(
        kernel,
        in_specs=in_specs,
        out_specs=out_specs if many else out_specs[0],
        out_shape=out_shape,
        scratch_shapes=scratch,
        name=name,
        cost_estimate=pl.CostEstimate(
            flops=int(micros * 1e8), bytes_accessed=int(micros * 3.5e6), transcendentals=0
        ),
        compiler_params=pltpu.CompilerParams(vmem_limit_bytes=VMEM_LIMIT),
    )


def from_behind(block, axis, distance):
    count = lax.axis_size(axis)
    return lax.ppermute(block, axis, [((i - distance) % count, i) for i in range(count)])


def per_device(orbitals, projections, aug_blocks, atom_home):
    n_band = lax.axis_size("band")
    n_slab = lax.axis_size("slab")
    owners = n_band * n_slab
    atom_dev = aug_blocks.shape[0]
    right, left, left_y, left_y_back = (jnp.asarray(t) for t in tables())
    squares = fold_square_host()


    messages = call(
        message_kernel,
        [vmem()],
        jax.ShapeDtypeStruct((n_band, CHANNEL_ROWS, NG), BF),
        [pltpu.VMEM((CHANNEL_ROWS, projections.shape[2]), F32)],
        "messages",
        1,
    )(projections)
    all_proj = lax.all_to_all(
        messages, "band", split_axis=0, concat_axis=0, tiled=True, axis_index_groups=[list(range(n_band))]
    )

    home_rows = atom_home.shape[1] // NG
    blocks, places, here, goes = call(
        local_kernel,
        [pl.BlockSpec(memory_space=pl.ANY), hbm(), vmem()],
        [
            jax.ShapeDtypeStruct((8, atom_dev * CHANNEL_ROWS, NG), BF),
            jax.ShapeDtypeStruct((home_rows, NG), jnp.int32),
            jax.ShapeDtypeStruct((home_rows, NG), F32),
            jax.ShapeDtypeStruct((atom_dev, NG), F32),
        ],
        [pltpu.VMEM((8, atom_dev * CHANNEL_ROWS, NG), F32)] * 2
        + [pltpu.VMEM(atom_home.shape, jnp.int32), pltpu.SemaphoreType.DMA],
        "local",
        1,
    )(messages, atom_home, aug_blocks.transpose(0, 2, 1, 3))
    own = orbitals
    proj, blocks = lax.optimization_barrier((projections, blocks))
    prev_proj = from_behind(proj, "band", 1)
    prev = from_behind(own, "band", 1)

    charges = call(
        charge_kernel,
        [vmem()] * 3,
        jax.ShapeDtypeStruct((owners, 16, NG), jnp.int16),
        [pltpu.VMEM((owners, 16, NG), jnp.int16), pltpu.SemaphoreType.DMA((4,))],
        "charges",
        2,
        [hbm()],
    )(goes, all_proj, blocks)
    charges = lax.all_to_all(charges, ("band", "slab"), split_axis=0, concat_axis=0, tiled=True)

    fold_y = jnp.asarray(squares[row_order()])
    fold_x = jnp.asarray(np.broadcast_to(squares[:, None], (NG, NG)).copy())
    fold_z = jnp.asarray(squares[None, :])

    def density(p, other, other_proj):
        return call(
            functools.partial(density_kernel, p),
            [vmem()] * 9,
            jax.ShapeDtypeStruct((n_slab, FWD_TILES, 16, NG), jnp.int16),
            [
                pltpu.VMEM((PLANES, NG, NG), F32),
                pltpu.VMEM((PLANES, NG, NG), F32),
                pltpu.VMEM((owners, NG), F32),
                pltpu.SMEM(places.shape, jnp.int32),
                pltpu.SemaphoreType.DMA,
            ],
            "density" + str(p),
            6,
        )(places, here, charges, own, other, proj, other_proj, right, left_y)

    def solve(name, base, spectrum, *more):
        tiles = BACK_TILES + FWD_TILES * len(more)
        return call(
            functools.partial(solve_kernel, base),
            [vmem()] * (3 + len(more)),
            jax.ShapeDtypeStruct((n_slab, tiles, 16, NG), jnp.int16),
            [pltpu.VMEM((ROWS, NG, NG), F32)],
            name,
            3,
        )(spectrum, table, left, *more)

    def swap(block):
        return lax.all_to_all(
            block, "slab", split_axis=0, concat_axis=0, tiled=True, axis_index_groups=[list(ROUND)]
        )

    cross = swap(density(1, prev, prev_proj))
    mine = density(0, own, proj)
    table = call(
        table_kernel,
        [pl.BlockSpec(memory_space=pl.ANY)] + [vmem()] * 3,
        jax.ShapeDtypeStruct((ROWS, NG, NG), F32),
        [],
        "table",
        1,
    )(mine, fold_y, fold_x, fold_z)
    cross = swap(solve("solve1", 0, cross, mine))
    mine = swap(solve("solve0", BACK_TILES, cross))

    kept, sent = call(
        back_cross_kernel,
        [vmem()] * 5,
        [
            jax.ShapeDtypeStruct((PLANES, NG, NG), F32),
            jax.ShapeDtypeStruct((PLANES * NG + PLANES, NG), jnp.int16),
        ],
        [pltpu.VMEM((PLANES, NG), F32)],
        "back_cross",
        2,
    )(cross, own, prev, left_y_back, right)
    got = from_behind(sent, "band", -1)
    return call(
        back_own_kernel,
        [vmem()] * 6,
        jax.ShapeDtypeStruct((1, PLANES, NG, NG), F32),
        [pltpu.VMEM((PLANES, NG, NG), F32), pltpu.SemaphoreType.DMA((PLANES // 2,))],
        "back_own",
        2,
        [hbm()],
    )(mine, own, kept, got, left_y_back, right)


def solution(mesh):
    in_specs = (
        P("band", "slab", None, None),
        P("band", None, None),
        P(("band", "slab"), None, None, None),
        P(),
    )
    out_specs = P("band", "slab", None, None)
    return jax.shard_map(
        per_device, mesh=mesh, in_specs=in_specs, out_specs=out_specs, check_vma=False
    )
```

```python
import functools
import math

import numpy as np
import jax
import jax.numpy as jnp
from jax import lax
from jax.experimental import pallas as pl
from jax.experimental.pallas import tpu as pltpu
from jax.sharding import PartitionSpec as P

KERNEL_SCALE = 0.5
SCREENING_RANGE = 0.002
NG = 128
SLABS = 8
ROWS = NG // SLABS
PLANES = NG // SLABS
BLOCK_LIMIT = 3.0
QMAX = 32760.0
STEPS = 8.0
CHANNEL_ROWS = 16
ROUND = (0, 1, 2, 3, 4, 5, 6, 7)
FWD_TILES = PLANES + 2
BACK_TILES = PLANES + 1
BF = jnp.bfloat16
F32 = jnp.float32
VMEM_LIMIT = 50 * 1024 * 1024


def hartley_host():
    index = np.arange(NG)
    angle = (index[:, None] * index[None, :] % NG) * (2.0 * math.pi / NG)
    return (np.cos(angle) + np.sin(angle)).astype(np.float32)


def split_host(table):
    high = table.astype(jnp.bfloat16)
    low = (table - high.astype(np.float32)).astype(jnp.bfloat16)
    return high, low


def row_order():
    by_size = sorted(range(NG), key=lambda k: (min(k, NG - k), k))
    return np.array([[by_size[d + SLABS * r] for r in range(ROWS)] for d in range(SLABS)])


def fold_square_host():
    index = np.arange(NG)
    return ((np.minimum(index, NG - index)).astype(np.float32) * np.float32(2.0 * math.pi / NG)) ** 2


def tables():
    table = hartley_host()
    high, low = split_host(table)
    order = row_order()[list(ROUND)].reshape(-1)
    high_y, low_y = high[order], low[order]
    top = np.concatenate([high, low], axis=1)
    bottom = np.concatenate([high, np.zeros_like(high)], axis=1)
    right = np.concatenate([top, bottom], axis=0)
    left = np.concatenate([high, low, high], axis=1)
    left_y = np.concatenate([high_y, low_y, high_y], axis=1)
    left_y_back = np.concatenate([high_y.T, low_y.T, high_y.T], axis=1)
    return right, left, left_y, left_y_back


def split(value):
    high = value.astype(BF)
    low = (value - high.astype(F32)).astype(BF)
    return high, low


def dot(a, b):
    return jnp.dot(a, b, preferred_element_type=F32)


def times_right(value, right_ref):
    high, low = split(value)
    both = dot(jnp.concatenate([high, low], axis=1), right_ref[...])
    return both[:, :NG] + both[:, NG:]


def times_left(left_ref, value):
    high, low = split(value)
    return dot(left_ref[...], jnp.concatenate([high, high, low], axis=0))


def step_code(largest):
    return jnp.ceil(jnp.log(jnp.maximum(largest, 1e-30)) * (STEPS / math.log(2.0)))


def step_size(code):
    return jnp.exp(code * (math.log(2.0) / STEPS)) * (1.001 / QMAX)


def to_int16(value):
    return value.astype(jnp.int32).astype(jnp.int16)


def from_int16(value):
    return value.astype(jnp.int32).astype(F32)


def local_kernel(after_ref, home_any, block_ref, out_ref, place_ref, here_ref, goes_ref, rows, turned, home_ref, sem):
    fetch = pltpu.make_async_copy(home_any, home_ref, sem)
    fetch.start()
    lane = lax.broadcasted_iota(jnp.int32, (1, NG), 1) // 8
    atoms, channels, bricks = block_ref.shape[:3]
    rows[...] = jnp.zeros_like(rows)
    for t in range(atoms):
        rows[:, pl.ds(CHANNEL_ROWS * t, channels), :] = jnp.swapaxes(block_ref[t].astype(F32), 0, 1)
    for k in range(bricks):
        values = rows[k]
        first = (k // 4) * 8 + (k // 2 % 2) * 2 + k % 2
        for back in range(12):
            moved = pltpu.roll(values, (first - back) % 16 * 8, 1)
            for x in range(2):
                y = back - 4 * x
                if 0 <= y < 8:
                    inside = lane == first + 4 * x
                    turned[y] = moved if k == 0 and x == 0 else jnp.where(inside, moved, turned[y])
    out_ref[...] = turned[...].astype(BF)
    fetch.wait()
    half = PLANES // 2
    slab = lax.axis_index("slab")
    here = home_ref[0:1, :] // half == slab
    place = (home_ref[0:1, :] - slab * half) * 2 + 16 * home_ref[1:2, :] + 256 * home_ref[2:3, :]
    place = jnp.where(here, place, 0)
    here = jnp.where(here, BLOCK_LIMIT / QMAX, 0.0)
    for r in range(place_ref.shape[0]):
        part = place[:, r * NG : (r + 1) * NG]
        total = part
        for t in range(1, atoms):
            total = total + pltpu.roll(part, NG - t, 1)
        place_ref[r : r + 1, :] = total
        here_ref[r : r + 1, :] = here[:, r * NG : (r + 1) * NG]
    owner = lax.axis_index("band") * SLABS + slab
    wide = home_ref.shape[1]
    mine = pltpu.roll(home_ref[0:1, :] // half, (wide - owner * atoms) & (wide - 1), 1)[:, :NG]
    slab_lane = lax.broadcasted_iota(jnp.int32, (1, NG), 1) & (SLABS - 1)
    for t in range(atoms):
        goes_ref[t : t + 1, :] = jnp.where(mine[:, t : t + 1] == slab_lane, 1.0, 0.0)


def message_kernel(proj_ref, out_ref, rows):
    rows[...] = jnp.zeros_like(rows)
    rows[pl.ds(0, proj_ref.shape[1]), :] = proj_ref[0].astype(F32)
    total = rows.shape[1]
    count = out_ref.shape[0]
    for b in range(count):
        moved = pltpu.roll(rows[...], (total - b * (total // count)) % total, 1)
        out_ref[b] = moved[:, :NG].astype(BF)


def streamed(out_ref, held, sems, chunk, start, size):
    part = pl.ds(start, size)
    copy = pltpu.make_async_copy(held.at[part], out_ref.at[part], sems.at[chunk])
    copy.start()
    return copy


def charge_kernel(goes_ref, proj_ref, block_ref, out_ref, held, sems):
    slab = lax.axis_index("slab")
    groups = proj_ref.shape[0]
    atoms = block_ref.shape[1] // CHANNEL_ROWS
    lane = lax.broadcasted_iota(jnp.int32, (CHANNEL_ROWS, NG), 1)
    weights = [jnp.zeros((CHANNEL_ROWS, NG), F32)] * atoms
    for b in range(groups):
        mine = pltpu.roll(proj_ref[b].astype(F32), (NG - slab * atoms) & (NG - 1), 1)
        for t in range(atoms):
            weights[t] = jnp.where(lane // SLABS == b, mine[:, t : t + 1], weights[t])
    pieces = []
    for t in range(atoms):
        behind = pltpu.roll(weights[t], SLABS, 1)
        picked = weights[t] * goes_ref[t : t + 1, :]
        pieces.append(jnp.concatenate([picked * weights[t], picked * behind], axis=1))
    weight = jnp.concatenate(pieces, axis=0)
    bound = jnp.sum(jnp.abs(weight), axis=0, keepdims=True) * BLOCK_LIMIT
    weight = jnp.transpose(weight * (QMAX / jnp.maximum(bound, 1e-30)))
    both = jnp.concatenate(split(weight), axis=1)
    half = weight.shape[0] // 2
    size = half // 4
    copies = []
    blocks = [jnp.concatenate([block_ref[y], block_ref[y]], axis=0) for y in range(8)]
    for n in range(4):
        pairs = []
        for p in range(2):
            rows = both[p * half + n * size : p * half + (n + 1) * size]
            values = jnp.round(jnp.stack([dot(rows, block) for block in blocks]))
            pairs.append(jnp.swapaxes(values, 0, 1))
        held[pl.ds(n * size, size)] = to_int16(jnp.concatenate(pairs, axis=1))
        copies.append(streamed(out_ref, held, sems, n, n * size, size))
    for copy in copies:
        copy.wait()


def density_kernel(p, place_vmem, here_ref, charge_ref, own_ref, prev_ref, proj_ref, prev_proj_ref, right_ref, left_ref, out_ref, field, second, scales, place_ref, sem, *stream):
    fetch = pltpu.make_async_copy(place_vmem, place_ref, sem)
    fetch.start()
    rows, owners = here_ref.shape[0], charge_ref.shape[0]
    count = owners // rows
    atoms = NG // count
    own_lane = lax.broadcasted_iota(jnp.int32, (count, NG), 1) // atoms == lax.broadcasted_iota(jnp.int32, (count, NG), 0)
    sizes = jnp.sum(jnp.abs(proj_ref[0].astype(F32) * prev_proj_ref[0].astype(F32)), axis=0, keepdims=True)
    for r in range(rows):
        bound = sizes[:, r * NG : (r + 1) * NG] * here_ref[r : r + 1, :]
        total = jnp.sum(jnp.where(own_lane, bound, 0.0), axis=1, keepdims=True)
        scales[pl.ds(r * count, count), :] = jnp.broadcast_to(total, (count, NG))
    for x in range(PLANES):
        field[x] = own_ref[0, x].astype(F32) * prev_ref[0, x].astype(F32)
    lane = lax.broadcasted_iota(jnp.int32, (8, NG), 1)
    fetch.wait()

    second[...] = jnp.zeros_like(second)

    def tiles_of(d, place, total):
        plane = place & 15
        brick_y = (place >> 4) & 15
        shift = (place >> 8) * 8
        inside = ((lane - shift) & (NG - 1)) < 16
        tile = from_int16(charge_ref[d])[8 * p : 8 * p + 8] * scales[pl.ds(d, 1), :]
        places = []
        for g in range(8):
            turned = pltpu.roll(tile, (shift + (NG - 16 * g)) & (NG - 1), 1)
            row = pl.multiple_of(((brick_y + g % 2) & (NG // 8 - 1)) * 8, 8)
            at = (plane + g // 2, pl.ds(row, 8))
            places.append((at, total[at] + jnp.where(inside, turned, 0.0)))
        return places

    def add_row(r, carry):
        for i in range(0, count, 2):
            pair = []
            for k, total in enumerate((field, second)):
                pair.append(tiles_of(r * count + i + k, place_ref[r, (i + k) * atoms], total))
            for places, total in zip(pair, (field, second)):
                for at, value in places:
                    total[at] = value
        return carry

    lax.fori_loop(0, rows, add_row, 0, unroll=True)
    for x in range(0, PLANES, 2):
        both = times_right(jnp.concatenate([field[x] + second[x], field[x + 1] + second[x + 1]], axis=0), right_ref)
        both = times_left(left_ref, jnp.concatenate([both[:NG], both[NG:]], axis=1))
        field[x] = both[:, :NG]
        field[x + 1] = both[:, NG:]

    packed = stream[0] if stream else out_ref
    copies = []
    for d in range(SLABS):
        rows = pl.ds(d * ROWS, ROWS)
        largest = jnp.abs(field[0, rows])
        for x in range(1, PLANES):
            largest = jnp.maximum(largest, jnp.abs(field[x, rows]))
        code = step_code(largest)
        factor = 1.0 / step_size(code)
        lows = []
        for x in range(PLANES):
            scaled = field[x, rows] * factor
            whole = jnp.round(scaled)
            packed[d, x] = to_int16(whole)
            lows.append((scaled - whole)[0:1])
        packed[d, PLANES] = to_int16(code)
        low = jnp.concatenate(lows, axis=0) * (2.0 * QMAX)
        packed[d, PLANES + 1] = to_int16(jnp.round(low))
        if stream:
            copies.append(streamed(out_ref, packed, stream[1], d, d, 1))
    for copy in copies:
        copy.wait()


def table_kernel(after_ref, squares_ref, fold_x_ref, fold_z_ref, out_ref):
    squares = squares_ref[pl.ds(lax.axis_index("slab"), 1), :]
    fold = fold_x_ref[...] + fold_z_ref[...]
    for r in range(ROWS):
        total = fold + squares[:, r : r + 1]
        out_ref[r] = jnp.where(total > 0, KERNEL_SCALE / (total + SCREENING_RANGE), 0.0) * (1.0 / NG**3)


def solve_kernel(base, in_ref, table_ref, left_ref, *rest):
    *more, out_ref, field = rest

    for s in range(SLABS):
        step = step_size(from_int16(in_ref[s, base + PLANES]))
        planes = from_int16(in_ref[s, pl.ds(base, PLANES)]) * step[None]
        low = from_int16(in_ref[s, base + PLANES + 1]) * (step[0:1] * (0.5 / QMAX))
        rows = pl.ds(ROUND[s] * PLANES, PLANES)
        field[:, rows, :] = jnp.swapaxes(planes, 0, 1)
        field[0, rows, :] = field[0, rows, :] + low
    for r in range(0, ROWS, 2):
        columns = jnp.concatenate([field[r], field[r + 1]], axis=1)
        spectrum = times_left(left_ref, columns) * jnp.concatenate([table_ref[r], table_ref[r + 1]], axis=1)
        columns = times_left(left_ref, spectrum)
        field[r] = columns[:, :NG]
        field[r + 1] = columns[:, NG:]
    for s in range(SLABS):
        planes = jnp.swapaxes(field[:, pl.ds(ROUND[s] * PLANES, PLANES), :], 0, 1)
        code = step_code(jnp.max(jnp.abs(planes), axis=0))
        out_ref[s, pl.ds(0, PLANES)] = to_int16(jnp.round(planes * (1.0 / step_size(code))[None]))
        out_ref[s, PLANES] = to_int16(code)
        for more_ref in more:
            out_ref[s, pl.ds(BACK_TILES, FWD_TILES)] = more_ref[s]


def potential_pair(in_ref, steps, x, left_ref, right_ref):
    halves = []
    for k in range(2):
        halves.append(jnp.concatenate([from_int16(in_ref[s, x + k]) * steps[s] for s in range(SLABS)], axis=0))
    both = times_left(left_ref, jnp.concatenate(halves, axis=1))
    both = times_right(jnp.concatenate([both[:, :NG], both[:, NG:]], axis=0), right_ref)
    return both[:NG], both[NG:]


def back_cross_kernel(in_ref, own_ref, prev_ref, left_ref, right_ref, kept_ref, sent_ref, codes):
    steps = [step_size(from_int16(in_ref[s, PLANES])) for s in range(SLABS)]
    for x in range(0, PLANES, 2):
        pair = potential_pair(in_ref, steps, x, left_ref, right_ref)
        for k in range(2):
            potential = pair[k]
            kept_ref[x + k] = potential * prev_ref[0, x + k].astype(F32)
            product = potential * own_ref[0, x + k].astype(F32)
            code = step_code(jnp.max(jnp.abs(product), axis=0, keepdims=True))
            codes[x + k : x + k + 1, :] = code
            sent_ref[pl.ds((x + k) * NG, NG), :] = to_int16(jnp.round(product * (1.0 / step_size(code))))
    sent_ref[pl.ds(PLANES * NG, PLANES), :] = to_int16(codes[...])


def back_own_kernel(in_ref, own_ref, kept_ref, sent_ref, left_ref, right_ref, out_ref, held, sems):
    copies = []
    steps = [step_size(from_int16(in_ref[s, PLANES])) for s in range(SLABS)]
    sent_steps = step_size(from_int16(sent_ref[pl.ds(PLANES * NG, PLANES), :]))
    for x in range(0, PLANES, 2):
        pair = potential_pair(in_ref, steps, x, left_ref, right_ref)
        for k in range(2):
            sent = from_int16(sent_ref[pl.ds((x + k) * NG, NG), :]) * sent_steps[x + k : x + k + 1]
            held[x + k] = kept_ref[x + k] + sent + pair[k] * own_ref[0, x + k].astype(F32)
        copies.append(streamed(out_ref.at[0], held, sems, x // 2, x, 2))
    for copy in copies:
        copy.wait()


def hbm():
    return pl.BlockSpec(memory_space=pltpu.HBM)


def vmem():
    return pl.BlockSpec(memory_space=pltpu.VMEM)


def smem():
    return pl.BlockSpec(memory_space=pltpu.SMEM)


def call(kernel, in_specs, out_shape, scratch, name, micros, out_specs=None):
    many = isinstance(out_shape, (list, tuple))
    out_specs = out_specs or [vmem()] * (len(out_shape) if many else 1)
    return pl.pallas_call(
        kernel,
        in_specs=in_specs,
        out_specs=out_specs if many else out_specs[0],
        out_shape=out_shape,
        scratch_shapes=scratch,
        name=name,
        cost_estimate=pl.CostEstimate(
            flops=int(micros * 1e8), bytes_accessed=int(micros * 3.5e6), transcendentals=0
        ),
        compiler_params=pltpu.CompilerParams(vmem_limit_bytes=VMEM_LIMIT),
    )


def from_behind(block, axis, distance):
    count = lax.axis_size(axis)
    return lax.ppermute(block, axis, [((i - distance) % count, i) for i in range(count)])


def per_device(orbitals, projections, aug_blocks, atom_home):
    n_band = lax.axis_size("band")
    n_slab = lax.axis_size("slab")
    owners = n_band * n_slab
    atom_dev = aug_blocks.shape[0]
    right, left, left_y, left_y_back = (jnp.asarray(t) for t in tables())
    squares = fold_square_host()


    messages = call(
        message_kernel,
        [vmem()],
        jax.ShapeDtypeStruct((n_band, CHANNEL_ROWS, NG), BF),
        [pltpu.VMEM((CHANNEL_ROWS, projections.shape[2]), F32)],
        "messages",
        1,
    )(projections)
    all_proj = lax.all_to_all(
        messages, "band", split_axis=0, concat_axis=0, tiled=True, axis_index_groups=[list(range(n_band))]
    )

    home_rows = atom_home.shape[1] // NG
    blocks, places, here, goes = call(
        local_kernel,
        [pl.BlockSpec(memory_space=pl.ANY), hbm(), vmem()],
        [
            jax.ShapeDtypeStruct((8, atom_dev * CHANNEL_ROWS, NG), BF),
            jax.ShapeDtypeStruct((home_rows, NG), jnp.int32),
            jax.ShapeDtypeStruct((home_rows, NG), F32),
            jax.ShapeDtypeStruct((atom_dev, NG), F32),
        ],
        [pltpu.VMEM((8, atom_dev * CHANNEL_ROWS, NG), F32)] * 2
        + [pltpu.VMEM(atom_home.shape, jnp.int32), pltpu.SemaphoreType.DMA],
        "local",
        1,
    )(messages, atom_home, aug_blocks.transpose(0, 2, 1, 3))
    own = orbitals
    proj, blocks = lax.optimization_barrier((projections, blocks))
    prev_proj = from_behind(proj, "band", 1)
    prev = from_behind(own, "band", 1)

    charges = call(
        charge_kernel,
        [vmem()] * 3,
        jax.ShapeDtypeStruct((owners, 16, NG), jnp.int16),
        [pltpu.VMEM((owners, 16, NG), jnp.int16), pltpu.SemaphoreType.DMA((4,))],
        "charges",
        2,
        [hbm()],
    )(goes, all_proj, blocks)
    charges = lax.all_to_all(charges, ("band", "slab"), split_axis=0, concat_axis=0, tiled=True)

    fold_y = jnp.asarray(squares[row_order()])
    fold_x = jnp.asarray(np.broadcast_to(squares[:, None], (NG, NG)).copy())
    fold_z = jnp.asarray(squares[None, :])

    def density(p, other, other_proj):
        shape = (n_slab, FWD_TILES, 16, NG)
        stream = [pltpu.VMEM(shape, jnp.int16), pltpu.SemaphoreType.DMA((SLABS,))] if p == 1 else []
        return call(
            functools.partial(density_kernel, p),
            [vmem()] * 9,
            jax.ShapeDtypeStruct((n_slab, FWD_TILES, 16, NG), jnp.int16),
            [
                pltpu.VMEM((PLANES, NG, NG), F32),
                pltpu.VMEM((PLANES, NG, NG), F32),
                pltpu.VMEM((owners, NG), F32),
                pltpu.SMEM(places.shape, jnp.int32),
                pltpu.SemaphoreType.DMA,
            ]
            + stream,
            "density" + str(p),
            6,
            [hbm()] if stream else None,
        )(places, here, charges, own, other, proj, other_proj, right, left_y)

    def solve(name, base, spectrum, *more):
        tiles = BACK_TILES + FWD_TILES * len(more)
        return call(
            functools.partial(solve_kernel, base),
            [vmem()] * (3 + len(more)),
            jax.ShapeDtypeStruct((n_slab, tiles, 16, NG), jnp.int16),
            [pltpu.VMEM((ROWS, NG, NG), F32)],
            name,
            3,
        )(spectrum, table, left, *more)

    def swap(block):
        return lax.all_to_all(
            block, "slab", split_axis=0, concat_axis=0, tiled=True, axis_index_groups=[list(ROUND)]
        )

    cross = swap(density(1, prev, prev_proj))
    mine = density(0, own, proj)
    table = call(
        table_kernel,
        [pl.BlockSpec(memory_space=pl.ANY)] + [vmem()] * 3,
        jax.ShapeDtypeStruct((ROWS, NG, NG), F32),
        [],
        "table",
        1,
    )(mine, fold_y, fold_x, fold_z)
    cross = swap(solve("solve1", 0, cross, mine))
    mine = swap(solve("solve0", BACK_TILES, cross))

    kept, sent = call(
        back_cross_kernel,
        [vmem()] * 5,
        [
            jax.ShapeDtypeStruct((PLANES, NG, NG), F32),
            jax.ShapeDtypeStruct((PLANES * NG + PLANES, NG), jnp.int16),
        ],
        [pltpu.VMEM((PLANES, NG), F32)],
        "back_cross",
        2,
    )(cross, own, prev, left_y_back, right)
    got = from_behind(sent, "band", -1)
    return call(
        back_own_kernel,
        [vmem()] * 6,
        jax.ShapeDtypeStruct((1, PLANES, NG, NG), F32),
        [pltpu.VMEM((PLANES, NG, NG), F32), pltpu.SemaphoreType.DMA((PLANES // 2,))],
        "back_own",
        2,
        [hbm()],
    )(mine, own, kept, got, left_y_back, right)


def solution(mesh):
    in_specs = (
        P("band", "slab", None, None),
        P("band", None, None),
        P(("band", "slab"), None, None, None),
        P(),
    )
    out_specs = P("band", "slab", None, None)
    return jax.shard_map(
        per_device, mesh=mesh, in_specs=in_specs, out_specs=out_specs, check_vma=False
    )
```
